128 devices in a mesh: band: 8 (over z, y_hi), fft: 16 (over y_lo, x, core).
Axes of the slice: x: 4, y: 4 (y_hi: 2, y_lo: 2; y = y_hi * 2 + y_lo), z: 4, core: 2. Of those that a mesh axis runs over, the one named last changes fastest.
Arguments:
- coeffs: bfloat16 [8, 384, 64, 2, 256], P('band', 'fft'), may hold values from -6 to 6
- potential: float32 [256, 256, 256], P('fft'), may hold values from -1 to 3
- pattern: int32 [384], replicated, may hold values from 0 to 1023, as said below
Outputs:
- images: bfloat16 [8, 384, 64, 2, 256], P('band', 'fft')
- matrix: float32 [2, 8, 8], P(None, 'band')
The draws below stay inside these ranges and needn't reach their ends.
Inputs may be any that keep to these rules, and one draw needn't show every extreme that they name: `pattern`: 384 distinct stick-block numbers; block b covers the xy positions b * 64 to b * 64 + 64 - 1 (x = position // 256, y = position % 256); entry m belongs to the coefficient block m, held by fft index m // 24.
All inputs are finite; a program needn't handle non-finite values.
Results may differ from the reference program's by a relative error of at most 0.01.
Values may be sent and summed in bfloat16 or wider, within the bound.
No kernel may reach another device: no remote copies, remote signals or barrier semaphores. Data moves between devices by JAX's collectives and lax.ppermute only.
A program may use at most 128 MiB of HBM per device.

```python
import math
import jax
import jax.numpy as jnp
from jax import lax

N = 256
SBW = 64
NBLK = 384
NB_ALL = 1024
BANDS = 8


well_count = 4


def sphere_blocks(key):
    key = jax.random.fold_in(key, 7)
    blocks = jnp.arange(NB_ALL, dtype=jnp.int32)
    start = blocks * SBW
    xpos = start // N
    ybase = start % N
    xdist = jnp.minimum(xpos, N - xpos)
    ydist = jnp.maximum(jnp.minimum(ybase, N - ybase - SBW), 0)
    score = xdist * xdist + ydist * ydist
    jitter = jax.random.randint(jax.random.fold_in(key, 3), (NB_ALL,), 0, N * N // 4, dtype=jnp.int32)
    ties = jax.random.permutation(jax.random.fold_in(key, 1), NB_ALL).astype(jnp.int32)
    ranked = (score + jitter) * NB_ALL + ties
    chosen = jnp.argsort(ranked, stable=True)[:NBLK].astype(jnp.int32)
    order = jax.random.permutation(jax.random.fold_in(key, 2), NBLK)
    return chosen[order].astype(jnp.int32)


def well_spots(key):
    spot_key = jax.random.fold_in(key, 5)
    return jax.random.randint(spot_key, (well_count, 3), 0, N, dtype=jnp.int32)


def draw_pattern(key, part):
    return sphere_blocks(key)


def draw_coeffs(key, part):
    blocks = sphere_blocks(key)
    spots = well_spots(key)
    key = jax.random.fold_in(key, 11)
    positions = blocks[:, None] * SBW + jnp.arange(SBW, dtype=jnp.int32)[None, :]
    xfreq = (positions // N)[:, :, None]
    yfreq = (positions % N)[:, :, None]
    kfreq = jnp.arange(N, dtype=jnp.int32)[None, None, :]
    phase_list = []
    for which in range(well_count):
        index = (xfreq * spots[which, 1] + yfreq * spots[which, 2] + kfreq * spots[which, 0]) % N
        phase_list.append(index.astype(jnp.float32) * (2.0 * math.pi / N))
    phases = jnp.stack(phase_list, axis=0)
    radii = jax.random.uniform(jax.random.fold_in(key, 1), (BANDS, well_count), jnp.float32, 0.25, 0.75)
    turns = jax.random.uniform(jax.random.fold_in(key, 2), (BANDS, well_count), jnp.float32, -math.pi, math.pi)

    def one_band(pair):
        radius, turn = pair
        offset = turn[:, None, None, None] - phases
        real_part = jnp.sum(radius[:, None, None, None] * jnp.cos(offset), axis=0)
        imag_part = jnp.sum(radius[:, None, None, None] * jnp.sin(offset), axis=0)
        return jnp.stack([real_part, imag_part], axis=2) * math.sqrt(2.0)
    shared = lax.map(one_band, (radii, turns))
    noise_key = jax.random.fold_in(key, 3)
    own = jnp.clip(jax.random.normal(noise_key, (BANDS, NBLK, SBW, 2, N), jnp.float32), -4.0, 4.0)
    mixed = 0.7 * shared + 0.7 * own
    return jnp.clip(mixed, -6.0, 6.0).astype(jnp.bfloat16)


def draw_potential(key, part):
    spots = well_spots(key)
    key = jax.random.fold_in(key, 13)
    base = jax.random.uniform(key, (N, N, N), jnp.float32, 0.5, 3.0)
    coords = jnp.arange(N, dtype=jnp.float32)
    spread = N / 16.0
    wells = jnp.zeros((N, N, N), jnp.float32)
    for which in range(well_count):
        profiles = []
        for axis_index in range(3):
            dist = jnp.abs(coords - spots[which, axis_index].astype(jnp.float32))
            dist = jnp.minimum(dist, N - dist)
            profiles.append(jnp.exp(-dist * dist / (2.0 * spread * spread)))
        depth = 0.5 * which
        wells = wells + depth * profiles[0][:, None, None] * profiles[1][None, :, None] * profiles[2][None, None, :]
    return jnp.maximum(base - wells, -1.0)


def setup_inputs(seed: int = 0) -> dict:
    keys = jax.random.split(jax.random.key(seed), 4)
    return {
        "coeffs": draw_coeffs(jax.random.fold_in(keys[3], 71), 0),
        "potential": draw_potential(jax.random.fold_in(keys[3], 71), 0),
        "pattern": draw_pattern(jax.random.fold_in(keys[3], 71), 0),
    }


def dft_table(grid_size, sign_value):
    counter = jnp.arange(grid_size, dtype=jnp.int32)
    phase_index = counter[:, None] * counter[None, :] % grid_size
    angles = phase_index.astype(jnp.float32) * (2.0 * math.pi / grid_size)
    unit_scale = 1.0 / math.sqrt(grid_size)
    cosine = jnp.cos(angles) * unit_scale
    sine_part = sign_value * jnp.sin(angles) * unit_scale
    upper_half = jnp.stack([cosine, sine_part], axis=1)
    lower_half = jnp.stack([-sine_part, cosine], axis=1)
    return jnp.stack([upper_half, lower_half], axis=0).astype(jnp.bfloat16)

def reference(coeffs, potential, pattern):
    grid_size = coeffs.shape[-1]
    block_width = coeffs.shape[2]
    all_blocks = grid_size * grid_size // block_width
    forward = dft_table(grid_size, 1.0).astype(jnp.float32)
    backward = dft_table(grid_size, -1.0).astype(jnp.float32)

    def apply_one(band_field):
        sticks = jnp.einsum('msck,ckdz->dzms', band_field.astype(jnp.float32), forward).astype(jnp.bfloat16)
        filled = jnp.zeros((2, grid_size, all_blocks, block_width), jnp.bfloat16)
        filled = filled.at[:, :, pattern].set(sticks).reshape(2, grid_size, grid_size, grid_size)
        along_y = jnp.einsum('czxy,cydw->dzxw', filled.astype(jnp.float32), forward).astype(jnp.bfloat16)
        along_x = jnp.einsum('czxy,cxdw->dzwy', along_y.astype(jnp.float32), forward)
        scaled_field = (along_x * potential[None]).astype(jnp.bfloat16)
        back_x = jnp.einsum('czxy,cxdw->dzwy', scaled_field.astype(jnp.float32), backward).astype(jnp.bfloat16)
        back_y = jnp.einsum('czxy,cydw->dzxw', back_x.astype(jnp.float32), backward)
        picked = back_y.reshape(2, grid_size, all_blocks, block_width)[:, :, pattern].astype(jnp.bfloat16)
        return jnp.einsum('czms,czdk->msdk', picked.astype(jnp.float32), backward).astype(jnp.bfloat16)
    images = lax.map(apply_one, coeffs)

    def block_terms(pair):
        left = pair[0].astype(jnp.float32)
        right = pair[1].astype(jnp.float32)
        real_part = jnp.einsum('isn,jsn->ij', left[:, :, 0], right[:, :, 0]) + jnp.einsum('isn,jsn->ij', left[:, :, 1], right[:, :, 1])
        imag_part = jnp.einsum('isn,jsn->ij', left[:, :, 0], right[:, :, 1]) - jnp.einsum('isn,jsn->ij', left[:, :, 1], right[:, :, 0])
        return jnp.stack([real_part, imag_part], axis=0)
    partials = lax.map(block_terms, (jnp.swapaxes(coeffs, 0, 1), jnp.swapaxes(images, 0, 1)))
    total_count = coeffs.shape[1] * block_width * grid_size
    matrix = lax.optimization_barrier(jnp.sum(partials, axis=0)) / total_count
    return (images, matrix)
```

```python
import functools
import math

import jax
import jax.numpy as jnp
import ml_dtypes
import numpy as np
from jax import lax
from jax.experimental import pallas as pl
from jax.experimental.pallas import tpu as pltpu
from jax.sharding import PartitionSpec as P

F32 = jnp.float32
BF16 = jnp.bfloat16
AXES = ("band", "fft")
VMEM = pl.BlockSpec(memory_space=pltpu.VMEM)


def dft_table(size, sign):
    counter = np.arange(size)
    angles = (counter[:, None] * counter[None, :] % size) * (2.0 * math.pi / size)
    cosine = np.cos(angles) / math.sqrt(size)
    sine = sign * np.sin(angles) / math.sqrt(size)
    table = np.stack([np.stack([cosine, sine], 1), np.stack([-sine, cosine], 1)], 0)
    return table.astype(ml_dtypes.bfloat16)


def plane_table(size, bands, ffts):
    per_fft = size // ffts
    per_dev = per_fft // bands
    forward = dft_table(size, 1.0)
    p, b, f = np.meshgrid(np.arange(per_dev), np.arange(bands), np.arange(ffts), indexing="ij")
    z = (f * per_fft + b * per_dev + p).reshape(-1)
    return np.ascontiguousarray(forward[:, :, :, z].transpose(3, 2, 0, 1)).reshape(2 * size, 2 * size)


def split_table(size, parts, per_dev):
    width = size // parts
    forward = dft_table(size, 1.0).astype(np.float32)
    out = np.zeros((parts, 2, per_dev, width, 2, per_dev, width), np.float32)
    for s in range(parts):
        part = forward[:, :width, :, s::parts]
        for p in range(per_dev):
            out[s, :, p, :, :, p, :] = part
    side = 2 * per_dev * width
    return out.reshape(parts, side, side).astype(ml_dtypes.bfloat16)


def order_table(size, parts, per_dev):
    width = size // parts
    out = np.zeros((per_dev, size, parts, per_dev, width), np.float32)
    for p in range(per_dev):
        for y in range(size):
            out[p, y, y % parts, p, y // parts] = 1.0
    return out.reshape(per_dev * size, parts * per_dev * width).astype(ml_dtypes.bfloat16)


def dot(a, b):
    return jnp.dot(a, b, preferred_element_type=F32)


def dot_nt(a, b):
    return lax.dot_general(a, b, (((1,), (1,)), ((), ())), preferred_element_type=F32)


def to_planes_kernel(c_ref, t_ref, o_ref, scr):
    half = t_ref.shape[0] // 2
    blocks = scr.shape[0] // half
    low = lax.broadcasted_iota(jnp.int32, (half, 128), 1) < 64
    for g in range(blocks // 4):
        r = dot_nt(t_ref[...], c_ref[g * 256 : (g + 1) * 256, :])
        for h in range(2):
            a = r[:half, h * 128 : (h + 1) * 128]
            b = r[half:, h * 128 : (h + 1) * 128]
            m = g * 4 + h * 2
            scr[pl.ds(m, half, stride=blocks), :] = jnp.where(low, a, pltpu.roll(b, 64, 1))
            scr[pl.ds(m + 1, half, stride=blocks), :] = jnp.where(low, pltpu.roll(a, 64, 1), b)
    o_ref[...] = scr[...].astype(BF16)


def from_planes_kernel(x_ref, t_ref, o_ref, scr):
    half = t_ref.shape[0] // 2
    blocks = scr.shape[0] // half
    scr[...] = x_ref[...].astype(F32)
    for g in range(blocks // 4):
        rows = []
        for m in range(g * 4, g * 4 + 4):
            y = jnp.transpose(scr[pl.ds(m, half, stride=blocks), :]).astype(BF16)
            rows.append(jnp.concatenate([y[:64], y[64:]], axis=1))
        left = jnp.concatenate(rows, axis=0)
        o_ref[g * 256 : (g + 1) * 256, :] = dot(left, t_ref[...]).astype(BF16)


def prepare_kernel(row_ref, col_ref, v_ref, f_ref, b_ref, ord_ref, tx_ref, xt_ref, v4_ref):
    size = f_ref.shape[0] // 2
    count = row_ref.shape[1]

    def hot(code, iota, s, axis):
        turn = (s * ((code >> 1) & 3) + (code & 1)) & 3
        hit = iota == (code >> 3)
        real = jnp.where(turn == 0, 1.0, jnp.where(turn == 2, -1.0, 0.0))
        imag = jnp.where(turn == 1, 1.0, jnp.where(turn == 3, -1.0, 0.0))
        return jnp.concatenate(
            [jnp.where(hit, real, 0.0), jnp.where(hit, imag, 0.0)], axis=axis
        ).astype(BF16)

    rows = lax.broadcasted_iota(jnp.int32, (size, count), 0)
    cols = lax.broadcasted_iota(jnp.int32, (count, size), 1)
    for s in range(4):
        tx_ref[s * 2 * size : (s + 1) * 2 * size, :] = dot(
            b_ref[...], hot(row_ref[...], rows, s, 0)
        ).astype(BF16)
        xt_ref[:, s * 2 * size : (s + 1) * 2 * size] = dot(
            hot(col_ref[...], cols, s, 1), f_ref[...]
        ).astype(BF16)
    v = jnp.concatenate([v_ref[0], v_ref[1]], axis=1)
    high = v.astype(BF16)
    rest = (v - high.astype(F32)).astype(BF16)
    v4_ref[...] = dot(high, ord_ref[...]) + dot(rest, ord_ref[...])


def planes_kernel(r_ref, tx_ref, xt_ref, v4_ref, yf_ref, yb_ref, o_ref, h_scr):
    size = v4_ref.shape[0]

    def pair(i, carry):
        w = jnp.concatenate([r_ref[2 * i], r_ref[2 * i + 1]], axis=1)
        for s in range(4):
            g = dot(tx_ref[s * 2 * size : (s + 1) * 2 * size, :], w).astype(BF16)
            v = v4_ref[:, s * 128 : (s + 1) * 128]
            v = jnp.concatenate([v, v], axis=1)
            for j in range(2):
                left = jnp.concatenate(
                    [g[:size, j * 128 : (j + 1) * 128], g[size:, j * 128 : (j + 1) * 128]], axis=1
                )
                field = (dot(left, yf_ref[s]) * v).astype(BF16)
                back = dot(field, yb_ref[s]).astype(BF16)
                row = s * 2 * size
                h_scr[row : row + size, j * 128 : (j + 1) * 128] = back[:, :128]
                h_scr[row + size : row + 2 * size, j * 128 : (j + 1) * 128] = back[:, 128:]
        out = dot(xt_ref[...], h_scr[...]).astype(BF16)
        o_ref[2 * i] = out[:, :128]
        o_ref[2 * i + 1] = out[:, 128:]
        return carry

    lax.fori_loop(0, r_ref.shape[0] // 2, pair, 0)


def gram_kernel(r_ref, p_ref, o_ref, r_scr, p_scr):
    bands, count = r_ref.shape[0], r_ref.shape[1]
    rows = 2 * bands
    groups = count // 48
    for src, scr in ((r_ref, r_scr), (p_ref, p_scr)):
        for b in range(bands):
            v = src[b].astype(F32)
            for f in range(groups):
                for d in range(2):
                    start = (f * 2 + d) * 24
                    scr[pl.ds(f * 24 * rows + b * 2 + d, 24, stride=rows), :] = v[start : start + 24]
    total = jnp.zeros((rows, rows), F32)
    for q in range(groups):
        base = q * 24 * rows
        sides = []
        for scr in (r_scr, p_scr):
            v = scr[base : base + 24 * rows, :].astype(BF16)
            sides.append(jnp.concatenate([v[m * rows : (m + 1) * rows] for m in range(24)], axis=1))
        total = total + dot_nt(sides[0], sides[1])
    o_ref[...] = total


def call(kernel, out_shape, scratch, flops, args):
    read = sum(a.size * a.dtype.itemsize for a in args)
    written = sum(s.size * s.dtype.itemsize for s in jax.tree.leaves(out_shape))
    return pl.pallas_call(
        kernel,
        out_shape=out_shape,
        in_specs=[VMEM] * len(args),
        out_specs=jax.tree.map(lambda _: VMEM, out_shape),
        scratch_shapes=scratch,
        compiler_params=pltpu.CompilerParams(vmem_limit_bytes=32 * 2**20),
        cost_estimate=pl.CostEstimate(flops=flops, bytes_accessed=read + written, transcendentals=0),
    )(*args)


def body(coeffs, potential, pattern):
    block_count, block_width = coeffs.shape[1], coeffs.shape[2]
    size = coeffs.shape[-1]
    bands, ffts = lax.axis_size("band"), lax.axis_size("fft")
    devices = bands * ffts
    per_dev = size // devices
    sticks = block_count * block_width
    rows = 2 * block_count
    shape = jax.ShapeDtypeStruct

    table = jnp.asarray(plane_table(size, bands, ffts))
    forward = dft_table(size, 1.0).reshape(2 * size, 2 * size)
    y_forward = split_table(size, 4, per_dev)
    y_backward = np.ascontiguousarray(y_forward.transpose(0, 2, 1))

    sent = call(
        to_planes_kernel,
        shape((devices * rows, 128), BF16),
        [pltpu.VMEM((devices * rows, 128), F32)],
        2 * sticks * (2 * size) ** 2,
        (coeffs.reshape(sticks, 2 * size), table),
    )
    got = lax.all_to_all(
        sent.reshape(devices, rows, 128), AXES, split_axis=0, concat_axis=0, tiled=True
    )
    got = got.reshape(bands, ffts * rows, 128)

    order = pattern.reshape(ffts, 1, block_count) * 2 + jnp.arange(2, dtype=jnp.int32)[None, :, None]
    planes = lax.dynamic_slice_in_dim(potential, lax.axis_index("band") * per_dev, per_dev, 0)
    count = ffts * rows
    x_table, x_back, v4 = call(
        prepare_kernel,
        (
            shape((8 * size, count), BF16),
            shape((count, 8 * size), BF16),
            shape((size, per_dev * size), F32),
        ),
        [],
        2 * 2 * 4 * count * (2 * size) ** 2,
        (
            order.reshape(1, count),
            order.reshape(count, 1),
            planes,
            jnp.asarray(forward),
            jnp.asarray(np.ascontiguousarray(forward.T)),
            jnp.asarray(order_table(size, 4, per_dev)),
        ),
    )

    picked = call(
        planes_kernel,
        shape((bands, count, 128), BF16),
        [pltpu.VMEM((8 * size, 256), BF16)],
        2 * bands * 128 * 2 * 8 * size * count,
        (got, x_table, x_back, v4, jnp.asarray(y_forward), jnp.asarray(y_backward)),
    )
    returned = lax.all_to_all(
        picked.reshape(devices, rows, 128), AXES, split_axis=0, concat_axis=0, tiled=True
    )

    gram = call(
        gram_kernel,
        shape((2 * bands, 2 * bands), F32),
        [pltpu.VMEM((bands * count, 128), F32)] * 2,
        2 * 256 * bands * count * 128,
        (got, picked),
    )
    gram = gram.reshape(bands, 2, bands, 2)
    total = jnp.stack(
        [gram[:, 0, :, 0] + gram[:, 1, :, 1], gram[:, 0, :, 1] - gram[:, 1, :, 0]], axis=0
    )
    for axis, extent in (("fft", ffts), ("band", bands)):
        step = 1
        while step < extent:
            total = total + lax.ppermute(total, axis, [(i, i ^ step) for i in range(extent)])
            step *= 2
    matrix = total / (block_count * ffts * block_width * size)
    matrix_rows = lax.dynamic_slice_in_dim(matrix, lax.axis_index("band"), 1, 1)

    images = call(
        from_planes_kernel,
        shape((sticks, 2 * size), BF16),
        [pltpu.VMEM((devices * rows, 128), F32)],
        2 * sticks * (2 * size) ** 2,
        (returned.reshape(devices * rows, 128), table),
    )
    return (images.reshape(coeffs.shape), matrix_rows)


def solution(mesh):
    placed = (P("band", "fft", None, None, None), P("fft", None, None), P())
    return jax.shard_map(
        body,
        mesh=mesh,
        in_specs=placed,
        out_specs=(P("band", "fft", None, None, None), P(None, "band", None)),
        check_vma=False,
    )
```

```python
import math

import jax
import jax.numpy as jnp
import ml_dtypes
import numpy as np
from jax import lax
from jax.experimental import pallas as pl
from jax.experimental.pallas import tpu as pltpu
from jax.sharding import PartitionSpec as P

F32 = jnp.float32
BF16 = jnp.bfloat16
AXES = ("band", "fft")
VMEM = pl.BlockSpec(memory_space=pltpu.VMEM)
HBM = pl.BlockSpec(memory_space=pltpu.HBM)


def dft_table(size, sign):
    counter = np.arange(size)
    angles = (counter[:, None] * counter[None, :] % size) * (2.0 * math.pi / size)
    cosine = np.cos(angles) / math.sqrt(size)
    sine = sign * np.sin(angles) / math.sqrt(size)
    table = np.stack([np.stack([cosine, sine], 1), np.stack([-sine, cosine], 1)], 0)
    return table.astype(ml_dtypes.bfloat16)


def plane_table(size, bands, ffts):
    per_fft = size // ffts
    per_dev = per_fft // bands
    forward = dft_table(size, 1.0)
    p, b, f = np.meshgrid(np.arange(per_dev), np.arange(bands), np.arange(ffts), indexing="ij")
    z = (f * per_fft + b * per_dev + p).reshape(-1)
    return np.ascontiguousarray(forward[:, :, :, z].transpose(3, 2, 0, 1)).reshape(2 * size, 2 * size)


def split_table(size, parts, per_dev):
    width = size // parts
    forward = dft_table(size, 1.0).astype(np.float32)
    out = np.zeros((parts, 2, per_dev, width, 2, per_dev, width), np.float32)
    for s in range(parts):
        part = forward[:, :width, :, s::parts]
        for p in range(per_dev):
            out[s, :, p, :, :, p, :] = part
    side = 2 * per_dev * width
    return out.reshape(parts, side, side).astype(ml_dtypes.bfloat16)


def order_table(size, parts, per_dev):
    width = size // parts
    out = np.zeros((per_dev, size, parts, per_dev, width), np.float32)
    for p in range(per_dev):
        for y in range(size):
            out[p, y, y % parts, p, y // parts] = 1.0
    return out.reshape(per_dev * size, parts * per_dev * width).astype(ml_dtypes.bfloat16)


def dot(a, b):
    return jnp.dot(a, b, preferred_element_type=F32)


def dot_nt(a, b):
    return lax.dot_general(a, b, (((1,), (1,)), ((), ())), preferred_element_type=F32)


def to_planes_kernel(c_ref, t_ref, o_ref, scr):
    half = t_ref.shape[0] // 2
    blocks = scr.shape[0] // half
    low = lax.broadcasted_iota(jnp.int32, (half, 128), 1) < 64
    for g in range(blocks // 4):
        r = dot_nt(t_ref[...], c_ref[g * 256 : (g + 1) * 256, :])
        for h in range(2):
            a = r[:half, h * 128 : (h + 1) * 128]
            b = r[half:, h * 128 : (h + 1) * 128]
            m = g * 4 + h * 2
            scr[pl.ds(m, half, stride=blocks), :] = jnp.where(low, a, pltpu.roll(b, 64, 1))
            scr[pl.ds(m + 1, half, stride=blocks), :] = jnp.where(low, pltpu.roll(a, 64, 1), b)
    o_ref[...] = scr[...].astype(BF16)


def from_planes_kernel(x_ref, t_hbm, o_ref, m_ref, scr, table, sem):
    copy = pltpu.make_async_copy(t_hbm, table, sem)
    copy.start()
    half = t_hbm.shape[0] // 2
    blocks = scr.shape[0] // half
    rows = 2 * blocks
    total = jnp.zeros((8, 128), F32)
    for i in range(x_ref.shape[0]):
        scr[i * rows : (i + 1) * rows, :] = x_ref[i, :rows, :].astype(F32)
        total = total + x_ref[i, rows:, :].astype(F32)
    m_ref[...] = jnp.broadcast_to(total[0:1] + (total[1:2] + total[2:3]), (8, 128))
    copy.wait()
    for g in range(blocks // 4):
        parts = []
        for m in range(g * 4, g * 4 + 4):
            y = jnp.transpose(scr[pl.ds(m, half, stride=blocks), :]).astype(BF16)
            parts.append(jnp.concatenate([y[:64], y[64:]], axis=1))
        left = jnp.concatenate(parts, axis=0)
        o_ref[g * 256 : (g + 1) * 256, :] = dot(left, table[...]).astype(BF16)


def prepare_kernel(
    row_ref, col_ref, v_ref, f_ref, b_ref, ord_ref, tx_hbm, xt_hbm, v4_hbm, tx, xt, v4, sems
):
    size = f_ref.shape[0] // 2
    count = row_ref.shape[1]

    def hot(code, iota, s, axis):
        turn = (s * ((code >> 1) & 3) + (code & 1)) & 3
        hit = iota == (code >> 3)
        real = jnp.where(turn == 0, 1.0, jnp.where(turn == 2, -1.0, 0.0))
        imag = jnp.where(turn == 1, 1.0, jnp.where(turn == 3, -1.0, 0.0))
        return jnp.concatenate(
            [jnp.where(hit, real, 0.0), jnp.where(hit, imag, 0.0)], axis=axis
        ).astype(BF16)

    copies = []
    rows = lax.broadcasted_iota(jnp.int32, (size, count), 0)
    cols = lax.broadcasted_iota(jnp.int32, (count, size), 1)
    for s in range(4):
        part = slice(s * 2 * size, (s + 1) * 2 * size)
        tx[part, :] = dot(b_ref[...], hot(row_ref[...], rows, s, 0)).astype(BF16)
        copies.append(pltpu.make_async_copy(tx.at[part], tx_hbm.at[part], sems.at[s]))
        copies[-1].start()
        xt[:, part] = dot(hot(col_ref[...], cols, s, 1), f_ref[...]).astype(BF16)
    copies.append(pltpu.make_async_copy(xt, xt_hbm, sems.at[4]))
    copies[-1].start()
    v = jnp.concatenate([v_ref[0], v_ref[1]], axis=1)
    high = v.astype(BF16)
    rest = (v - high.astype(F32)).astype(BF16)
    both = dot(high, ord_ref[...]) + dot(rest, ord_ref[...])
    for s in range(4):
        v4[s] = both[:, s * 128 : (s + 1) * 128]
    copies.append(pltpu.make_async_copy(v4, v4_hbm, sems.at[5]))
    copies[-1].start()
    for copy in copies:
        copy.wait()


def planes_kernel(
    r_ref, tx_hbm, xt_hbm, v4_hbm, yf_ref, yb_ref, o_ref, tx, xt, v4, h, r_scr, p_scr, sems
):
    size = v4.shape[1]
    bands, count = r_ref.shape[0], r_ref.shape[1]
    ffts, blocks = o_ref.shape[1], count // (2 * o_ref.shape[1])
    rows, width = 2 * blocks, 2 * bands
    load_v = pltpu.make_async_copy(v4_hbm, v4, sems.at[5])
    loads = []
    for s in range(4):
        part = slice(s * 2 * size, (s + 1) * 2 * size)
        loads.append(pltpu.make_async_copy(tx_hbm.at[part], tx.at[part], sems.at[s]))
    load_xt = pltpu.make_async_copy(xt_hbm, xt, sems.at[4])
    loads[0].start()
    load_v.start()
    for copy in loads[1:]:
        copy.start()
    load_xt.start()

    def spread(scr, b, v):
        for f in range(ffts):
            for d in range(2):
                start = (f * 2 + d) * blocks
                at = pl.ds(f * blocks * width + d * bands + b, blocks, stride=width)
                scr[at, :] = v[start : start + blocks]

    for s in range(4):
        loads[s].wait()
        if s == 0:
            load_v.wait()
        w = jnp.concatenate([r_ref[b] for b in range(bands)], axis=1)
        g = dot(tx[s * 2 * size : (s + 1) * 2 * size, :], w).astype(BF16)
        left = jnp.concatenate(
            [
                jnp.concatenate(
                    [g[:size, b * 128 : (b + 1) * 128], g[size:, b * 128 : (b + 1) * 128]], axis=1
                )
                for b in range(bands)
            ],
            axis=0,
        )
        v = jnp.concatenate([v4[s], v4[s]], axis=1)
        field = (dot(left, yf_ref[s]) * jnp.concatenate([v] * bands, axis=0)).astype(BF16)
        back = dot(field, yb_ref[s]).astype(BF16)
        row = s * 2 * size
        for b in range(bands):
            part = back[b * size : (b + 1) * size]
            h[row : row + size, b * 128 : (b + 1) * 128] = part[:, :128]
            h[row + size : row + 2 * size, b * 128 : (b + 1) * 128] = part[:, 128:]
        for b in range(2 * s, 2 * s + 2):
            spread(r_scr, b, r_ref[b].astype(F32))
    load_xt.wait()
    for n in range(bands // 2):
        out = dot(xt[...], h[:, n * 256 : (n + 1) * 256])
        for j in range(2):
            b = 2 * n + j
            v = out[:, j * 128 : (j + 1) * 128]
            spread(p_scr, b, v)
            v = v.astype(BF16)
            for f in range(ffts):
                o_ref[b, f, :rows, :] = v[f * rows : (f + 1) * rows]

    gram = jnp.zeros((width, width), F32)
    for f in range(ffts):
        sides = []
        for scr in (r_scr, p_scr):
            v = scr[f * blocks * width : (f + 1) * blocks * width, :].astype(BF16)
            sides.append(
                jnp.concatenate([v[m * width : (m + 1) * width] for m in range(blocks)], axis=1)
            )
        gram = gram + dot_nt(sides[0], sides[1])
    real = gram[:bands, :bands] + gram[bands:, bands:]
    imag = gram[:bands, bands:] - gram[bands:, :bands]
    total = jnp.concatenate([real, imag, jnp.zeros((bands, 128 - width), F32)], axis=1)
    first = total.astype(BF16).astype(F32)
    second = (total - first).astype(BF16).astype(F32)
    third = total - first - second
    line = lax.broadcasted_iota(jnp.int32, (8, 128), 0)
    for b in range(bands):
        part = jnp.where(
            line == 0,
            first[b : b + 1],
            jnp.where(line == 1, second[b : b + 1], jnp.where(line == 2, third[b : b + 1], 0.0)),
        ).astype(BF16)
        for f in range(ffts):
            o_ref[b, f, rows:, :] = part


def call(kernel, out_shape, scratch, flops, args, in_hbm=(), out_hbm=False):
    read = sum(a.size * a.dtype.itemsize for a in args)
    written = sum(s.size * s.dtype.itemsize for s in jax.tree.leaves(out_shape))
    return pl.pallas_call(
        kernel,
        out_shape=out_shape,
        in_specs=[HBM if i in in_hbm else VMEM for i in range(len(args))],
        out_specs=jax.tree.map(lambda _: HBM if out_hbm else VMEM, out_shape),
        scratch_shapes=scratch,
        compiler_params=pltpu.CompilerParams(vmem_limit_bytes=40 * 2**20),
        cost_estimate=pl.CostEstimate(flops=flops, bytes_accessed=read + written, transcendentals=0),
    )(*args)


def body(coeffs, potential, pattern):
    block_count, block_width = coeffs.shape[1], coeffs.shape[2]
    size = coeffs.shape[-1]
    bands, ffts = lax.axis_size("band"), lax.axis_size("fft")
    devices = bands * ffts
    per_dev = size // devices
    sticks = block_count * block_width
    rows = 2 * block_count
    shape = jax.ShapeDtypeStruct

    table = jnp.asarray(plane_table(size, bands, ffts))
    forward = dft_table(size, 1.0).reshape(2 * size, 2 * size)
    y_forward = split_table(size, 4, per_dev)
    y_backward = np.ascontiguousarray(y_forward.transpose(0, 2, 1))

    sent = call(
        to_planes_kernel,
        shape((devices * rows, 128), BF16),
        [pltpu.VMEM((devices * rows, 128), F32)],
        2 * sticks * (2 * size) ** 2,
        (coeffs.reshape(sticks, 2 * size), table),
    )
    got = lax.all_to_all(
        sent.reshape(devices, rows, 128), AXES, split_axis=0, concat_axis=0, tiled=True
    )
    got = got.reshape(bands, ffts * rows, 128)

    order = pattern.reshape(ffts, 1, block_count) * 2 + jnp.arange(2, dtype=jnp.int32)[None, :, None]
    planes = lax.dynamic_slice_in_dim(potential, lax.axis_index("band") * per_dev, per_dev, 0)
    count = ffts * rows
    tables = (
        shape((8 * size, count), BF16),
        shape((count, 8 * size), BF16),
        shape((4, size, per_dev * size // 4), F32),
    )
    held = [pltpu.VMEM(t.shape, t.dtype) for t in tables]
    x_table, x_back, v4 = call(
        prepare_kernel,
        tables,
        held + [pltpu.SemaphoreType.DMA((6,))],
        2 * 2 * 4 * count * (2 * size) ** 2,
        (
            order.reshape(1, count),
            order.reshape(count, 1),
            planes,
            jnp.asarray(forward),
            jnp.asarray(np.ascontiguousarray(forward.T)),
            jnp.asarray(order_table(size, 4, per_dev)),
        ),
        out_hbm=True,
    )

    picked = call(
        planes_kernel,
        shape((bands, ffts, rows + 8, 128), BF16),
        held
        + [pltpu.VMEM((8 * size, bands * 128), BF16)]
        + [pltpu.VMEM((bands * count, 128), F32)] * 2
        + [pltpu.SemaphoreType.DMA((6,))],
        2 * bands * 128 * 2 * 8 * size * count,
        (got, x_table, x_back, v4, jnp.asarray(y_forward), jnp.asarray(y_backward)),
        in_hbm=(1, 2, 3),
    )
    returned = lax.all_to_all(
        picked.reshape(devices, rows + 8, 128), AXES, split_axis=0, concat_axis=0, tiled=True
    )

    images, sums = call(
        from_planes_kernel,
        (shape((sticks, 2 * size), BF16), shape((8, 128), F32)),
        [
            pltpu.VMEM((devices * rows, 128), F32),
            pltpu.VMEM((2 * size, 2 * size), BF16),
            pltpu.SemaphoreType.DMA(()),
        ],
        2 * sticks * (2 * size) ** 2,
        (returned, table),
        in_hbm=(1,),
    )
    matrix_rows = sums[0, : 2 * bands].reshape(2, 1, bands) / (block_count * ffts * block_width * size)
    return (images.reshape(coeffs.shape), matrix_rows)


def solution(mesh):
    placed = (P("band", "fft", None, None, None), P("fft", None, None), P())
    return jax.shard_map(
        body,
        mesh=mesh,
        in_specs=placed,
        out_specs=(P("band", "fft", None, None, None), P(None, "band", None)),
        check_vma=False,
    )
```

```python
import functools
import math

import jax
import jax.numpy as jnp
import ml_dtypes
import numpy as np
from jax import lax
from jax.experimental import pallas as pl
from jax.experimental.pallas import tpu as pltpu
from jax.sharding import PartitionSpec as P

F32 = jnp.float32
BF16 = jnp.bfloat16
AXES = ("band", "fft")
VMEM = pl.BlockSpec(memory_space=pltpu.VMEM)
HBM = pl.BlockSpec(memory_space=pltpu.HBM)


def dft_table(size, sign):
    counter = np.arange(size)
    angles = (counter[:, None] * counter[None, :] % size) * (2.0 * math.pi / size)
    cosine = np.cos(angles) / math.sqrt(size)
    sine = sign * np.sin(angles) / math.sqrt(size)
    table = np.stack([np.stack([cosine, sine], 1), np.stack([-sine, cosine], 1)], 0)
    return table.astype(ml_dtypes.bfloat16)


def plane_table(size, bands, ffts):
    per_fft = size // ffts
    per_dev = per_fft // bands
    forward = dft_table(size, 1.0)
    p, b, f = np.meshgrid(np.arange(per_dev), np.arange(bands), np.arange(ffts), indexing="ij")
    z = (f * per_fft + b * per_dev + p).reshape(-1)
    rows = forward[:, :, :, z].reshape(2, size, 2, per_dev, bands * ffts)
    return np.ascontiguousarray(rows.transpose(3, 2, 4, 0, 1)).reshape(2 * size, 2 * size)


def split_table(size, parts, per_dev):
    width = size // parts
    forward = dft_table(size, 1.0).astype(np.float32)
    out = np.zeros((parts, 2, per_dev, width, 2, per_dev, width), np.float32)
    for s in range(parts):
        part = forward[:, :width, :, s::parts]
        for p in range(per_dev):
            out[s, :, p, :, :, p, :] = part
    side = 2 * per_dev * width
    return out.reshape(parts, side, side).astype(ml_dtypes.bfloat16)


def order_table(size, parts, per_dev):
    width = size // parts
    out = np.zeros((per_dev, size, parts, per_dev, width), np.float32)
    for p in range(per_dev):
        for y in range(size):
            out[p, y, y % parts, p, y // parts] = 1.0
    return out.reshape(per_dev * size, parts * per_dev * width).astype(ml_dtypes.bfloat16)


def dot(a, b):
    return jnp.dot(a, b, preferred_element_type=F32)


def dot_nt(a, b):
    return lax.dot_general(a, b, (((1,), (1,)), ((), ())), preferred_element_type=F32)


def to_planes_kernel(c_ref, t_ref, o_ref, scr):
    half = t_ref.shape[0] // 2
    devices = half // 2
    rows = scr.shape[0] // devices
    blocks = rows // 2
    low = lax.broadcasted_iota(jnp.int32, (half, 128), 1) < 64
    for g in range(blocks // 4):
        r = dot_nt(t_ref[...], c_ref[g * 256 : (g + 1) * 256, :])
        for h in range(2):
            a = r[:half, h * 128 : (h + 1) * 128]
            b = r[half:, h * 128 : (h + 1) * 128]
            even = jnp.where(low, a, pltpu.roll(b, 64, 1))
            odd = jnp.where(low, pltpu.roll(a, 64, 1), b)
            for d in range(2):
                at = d * blocks + g * 4 + h * 2
                part = slice(d * devices, (d + 1) * devices)
                scr[pl.ds(at, devices, stride=rows), :] = even[part]
                scr[pl.ds(at + 1, devices, stride=rows), :] = odd[part]
    o_ref[...] = scr[...].astype(BF16)


def from_planes_kernel(count, x_ref, t_hbm, o_ref, m_ref, scr, table, sem):
    copy = pltpu.make_async_copy(t_hbm, table, sem)
    copy.start()
    devices = t_hbm.shape[0] // 4
    rows = scr.shape[0] // devices
    blocks = rows // 2 - 1
    bands = m_ref.shape[2]
    scr[...] = x_ref[...].astype(F32)
    line = jnp.sum(scr[pl.ds(2 * blocks, devices, stride=rows), :], axis=0, keepdims=True)
    width = 2 * bands
    total = line[:, :width] + (line[:, width : 2 * width] + line[:, 2 * width : 3 * width])
    total = total / count
    m_ref[0] = total[:, :bands]
    m_ref[1] = total[:, bands:]
    copy.wait()
    for g in range(blocks // 4):
        parts = []
        for m in range(g * 4, g * 4 + 4):
            y = jnp.concatenate(
                [scr[pl.ds(d * blocks + m, devices, stride=rows), :] for d in range(2)], axis=0
            )
            y = jnp.transpose(y).astype(BF16)
            parts.append(jnp.concatenate([y[:64], y[64:]], axis=1))
        left = jnp.concatenate(parts, axis=0)
        o_ref[g * 256 : (g + 1) * 256, :] = dot(left, table[...]).astype(BF16)


def prepare_kernel(
    row_ref, col_ref, v_ref, f_ref, b_ref, ord_ref, tx_hbm, xt_hbm, v4_hbm, tx, xt, v4, sems
):
    size = f_ref.shape[0] // 2
    count = row_ref.shape[1]

    def hot(code, iota, s, axis):
        turn = (s * ((code >> 1) & 3) + (code & 1)) & 3
        hit = iota == (code >> 3)
        real = jnp.where(turn == 0, 1.0, jnp.where(turn == 2, -1.0, 0.0))
        imag = jnp.where(turn == 1, 1.0, jnp.where(turn == 3, -1.0, 0.0))
        return jnp.concatenate(
            [jnp.where(hit, real, 0.0), jnp.where(hit, imag, 0.0)], axis=axis
        ).astype(BF16)

    copies = []
    rows = lax.broadcasted_iota(jnp.int32, (size, count), 0)
    cols = lax.broadcasted_iota(jnp.int32, (count, size), 1)
    for s in range(4):
        part = slice(s * 2 * size, (s + 1) * 2 * size)
        tx[part, :] = dot(b_ref[...], hot(row_ref[...], rows, s, 0)).astype(BF16)
        copies.append(pltpu.make_async_copy(tx.at[part], tx_hbm.at[part], sems.at[s]))
        copies[-1].start()
        xt[:, part] = dot(hot(col_ref[...], cols, s, 1), f_ref[...]).astype(BF16)
    copies.append(pltpu.make_async_copy(xt, xt_hbm, sems.at[4]))
    copies[-1].start()
    v = jnp.concatenate([v_ref[0], v_ref[1]], axis=1)
    high = v.astype(BF16)
    rest = (v - high.astype(F32)).astype(BF16)
    both = dot(high, ord_ref[...]) + dot(rest, ord_ref[...])
    for s in range(4):
        v4[s] = both[:, s * 128 : (s + 1) * 128]
    copies.append(pltpu.make_async_copy(v4, v4_hbm, sems.at[5]))
    copies[-1].start()
    for copy in copies:
        copy.wait()


def planes_kernel(
    groups, r_ref, tx_hbm, xt_hbm, v4_hbm, yf_ref, yb_ref, o_ref, tx, xt, v4, h, r_scr, p_scr, sems
):
    size = v4.shape[1]
    bands, count = r_ref.shape[0], r_ref.shape[1]
    ffts = sum(groups)
    rows, blocks = count // ffts, count // ffts // 2
    message = p_scr.shape[0] // (bands * ffts)
    width = 2 * bands
    load_v = pltpu.make_async_copy(v4_hbm, v4, sems.at[5])
    loads = []
    for s in range(4):
        part = slice(s * 2 * size, (s + 1) * 2 * size)
        loads.append(pltpu.make_async_copy(tx_hbm.at[part], tx.at[part], sems.at[s]))
    load_xt = pltpu.make_async_copy(xt_hbm, xt, sems.at[4])
    loads[0].start()
    load_v.start()
    for copy in loads[1:]:
        copy.start()
    load_xt.start()

    for s in range(4):
        loads[s].wait()
        if s == 0:
            load_v.wait()
        w = jnp.concatenate([r_ref[b] for b in range(bands)], axis=1)
        g = dot(tx[s * 2 * size : (s + 1) * 2 * size, :], w).astype(BF16)
        left = jnp.concatenate(
            [
                jnp.concatenate(
                    [g[:size, b * 128 : (b + 1) * 128], g[size:, b * 128 : (b + 1) * 128]], axis=1
                )
                for b in range(bands)
            ],
            axis=0,
        )
        v = jnp.concatenate([v4[s], v4[s]], axis=1)
        field = (dot(left, yf_ref[s]) * jnp.concatenate([v] * bands, axis=0)).astype(BF16)
        back = dot(field, yb_ref[s]).astype(BF16)
        row = s * 2 * size
        for b in range(bands):
            part = back[b * size : (b + 1) * size]
            h[row : row + size, b * 128 : (b + 1) * 128] = part[:, :128]
            h[row + size : row + 2 * size, b * 128 : (b + 1) * 128] = part[:, 128:]
        for b in range(2 * s, 2 * s + 2):
            r_scr[b * count : (b + 1) * count, :] = r_ref[b].astype(F32)

    def side(scr, start, stride):
        tiles = []
        for m in range(blocks):
            real = scr[pl.ds(start + m, bands, stride=stride), :]
            imag = scr[pl.ds(start + blocks + m, bands, stride=stride), :]
            tiles.append(jnp.concatenate([real, imag], axis=0).astype(BF16))
        return jnp.concatenate(tiles, axis=1)

    load_xt.wait()
    gram = jnp.zeros((width, width), F32)
    first = 0
    for group in groups:
        out = dot(xt[first * rows : (first + group) * rows, :], h[...])
        for f in range(first, first + group):
            for b in range(bands):
                at = (b * ffts + f) * message
                start = (f - first) * rows
                p_scr[at : at + rows, :] = out[start : start + rows, b * 128 : (b + 1) * 128]
        for f in range(first, first + group):
            left = side(r_scr, f * rows, count)
            gram = gram + dot_nt(left, side(p_scr, f * message, ffts * message))
        first += group

    real = gram[:bands, :bands] + gram[bands:, bands:]
    imag = gram[:bands, bands:] - gram[bands:, :bands]
    total = jnp.concatenate([real, imag], axis=1)
    high = total.astype(BF16).astype(F32)
    middle = (total - high).astype(BF16).astype(F32)
    low = total - high - middle
    lines = jnp.concatenate([high, middle, low, jnp.zeros((bands, 128 - 3 * width), F32)], axis=1)
    empty = jnp.zeros((message - rows - 1, 128), F32)
    for b in range(bands):
        part = jnp.concatenate([lines[b : b + 1], empty], axis=0)
        for f in range(ffts):
            at = (b * ffts + f) * message + rows
            p_scr[at : at + message - rows, :] = part
    o_ref[...] = p_scr[...].astype(BF16)


def call(kernel, out_shape, scratch, flops, args, in_hbm=(), out_hbm=False, limit=40):
    read = sum(a.size * a.dtype.itemsize for a in args)
    written = sum(s.size * s.dtype.itemsize for s in jax.tree.leaves(out_shape))
    return pl.pallas_call(
        kernel,
        out_shape=out_shape,
        in_specs=[HBM if i in in_hbm else VMEM for i in range(len(args))],
        out_specs=jax.tree.map(lambda _: HBM if out_hbm else VMEM, out_shape),
        scratch_shapes=scratch,
        compiler_params=pltpu.CompilerParams(vmem_limit_bytes=limit * 2**20),
        cost_estimate=pl.CostEstimate(flops=flops, bytes_accessed=read + written, transcendentals=0),
    )(*args)


def body(coeffs, potential, pattern):
    block_count, block_width = coeffs.shape[1], coeffs.shape[2]
    size = coeffs.shape[-1]
    bands, ffts = lax.axis_size("band"), lax.axis_size("fft")
    devices = bands * ffts
    per_dev = size // devices
    sticks = block_count * block_width
    rows = 2 * block_count
    shape = jax.ShapeDtypeStruct

    table = jnp.asarray(plane_table(size, bands, ffts))
    forward = dft_table(size, 1.0).reshape(2 * size, 2 * size)
    y_forward = split_table(size, 4, per_dev)
    y_backward = np.ascontiguousarray(y_forward.transpose(0, 2, 1))

    sent = call(
        to_planes_kernel,
        shape((devices * rows, 128), BF16),
        [pltpu.VMEM((devices * rows, 128), F32)],
        2 * sticks * (2 * size) ** 2,
        (coeffs.reshape(sticks, 2 * size), table),
    )
    got = lax.all_to_all(
        sent.reshape(devices, rows, 128), AXES, split_axis=0, concat_axis=0, tiled=True
    )
    got = got.reshape(bands, ffts * rows, 128)

    order = pattern.reshape(ffts, 1, block_count) * 2 + jnp.arange(2, dtype=jnp.int32)[None, :, None]
    planes = lax.dynamic_slice_in_dim(potential, lax.axis_index("band") * per_dev, per_dev, 0)
    count = ffts * rows
    tables = (
        shape((8 * size, count), BF16),
        shape((count, 8 * size), BF16),
        shape((4, size, per_dev * size // 4), F32),
    )
    held = [pltpu.VMEM(t.shape, t.dtype) for t in tables]
    x_table, x_back, v4 = call(
        prepare_kernel,
        tables,
        held + [pltpu.SemaphoreType.DMA((6,))],
        2 * 2 * 4 * count * (2 * size) ** 2,
        (
            order.reshape(1, count),
            order.reshape(count, 1),
            planes,
            jnp.asarray(forward),
            jnp.asarray(np.ascontiguousarray(forward.T)),
            jnp.asarray(order_table(size, 4, per_dev)),
        ),
        out_hbm=True,
        limit=57,
    )

    message = rows + 2
    picked = call(
        functools.partial(planes_kernel, (6, 5, 5)),
        shape((devices * message, 128), BF16),
        held
        + [pltpu.VMEM((8 * size, bands * 128), BF16)]
        + [pltpu.VMEM((bands * count, 128), F32), pltpu.VMEM((devices * message, 128), F32)]
        + [pltpu.SemaphoreType.DMA((6,))],
        2 * bands * 128 * 2 * 8 * size * count,
        (got, x_table, x_back, v4, jnp.asarray(y_forward), jnp.asarray(y_backward)),
        in_hbm=(1, 2, 3),
        limit=57,
    )
    returned = lax.all_to_all(
        picked.reshape(devices, message // 2, 2, 128), AXES, split_axis=0, concat_axis=0, tiled=True
    )

    total_count = block_count * ffts * block_width * size
    images, matrix_rows = call(
        functools.partial(from_planes_kernel, total_count),
        (shape((sticks, 2 * size), BF16), shape((2, 1, bands), F32)),
        [
            pltpu.VMEM((devices * message, 128), F32),
            pltpu.VMEM((2 * size, 2 * size), BF16),
            pltpu.SemaphoreType.DMA(()),
        ],
        2 * sticks * (2 * size) ** 2,
        (returned.reshape(devices * message, 128), table),
        in_hbm=(1,),
    )
    return (images.reshape(coeffs.shape), matrix_rows)


def solution(mesh):
    placed = (P("band", "fft", None, None, None), P("fft", None, None), P())
    return jax.shard_map(
        body,
        mesh=mesh,
        in_specs=placed,
        out_specs=(P("band", "fft", None, None, None), P(None, "band", None)),
        check_vma=False,
    )
```

```python
import functools
import math

import jax
import jax.numpy as jnp
import ml_dtypes
import numpy as np
from jax import lax
from jax.experimental import pallas as pl
from jax.experimental.pallas import tpu as pltpu
from jax.sharding import PartitionSpec as P

F32 = jnp.float32
BF16 = jnp.bfloat16
AXES = ("band", "fft")
VMEM = pl.BlockSpec(memory_space=pltpu.VMEM)
HBM = pl.BlockSpec(memory_space=pltpu.HBM)


def dft_table(size, sign):
    counter = np.arange(size)
    angles = (counter[:, None] * counter[None, :] % size) * (2.0 * math.pi / size)
    cosine = np.cos(angles) / math.sqrt(size)
    sine = sign * np.sin(angles) / math.sqrt(size)
    table = np.stack([np.stack([cosine, sine], 1), np.stack([-sine, cosine], 1)], 0)
    return table.astype(ml_dtypes.bfloat16)


def plane_table(size, bands, ffts):
    per_fft = size // ffts
    per_dev = per_fft // bands
    forward = dft_table(size, 1.0)
    p, b, f = np.meshgrid(np.arange(per_dev), np.arange(bands), np.arange(ffts), indexing="ij")
    z = (f * per_fft + b * per_dev + p).reshape(-1)
    rows = forward[:, :, :, z].reshape(2, size, 2, per_dev, bands * ffts)
    return np.ascontiguousarray(rows.transpose(3, 2, 4, 0, 1)).reshape(2 * size, 2 * size)


def split_table(size, parts, per_dev):
    width = size // parts
    forward = dft_table(size, 1.0).astype(np.float32)
    out = np.zeros((parts, 2, per_dev, width, 2, per_dev, width), np.float32)
    for s in range(parts):
        part = forward[:, :width, :, s::parts]
        for p in range(per_dev):
            out[s, :, p, :, :, p, :] = part
    side = 2 * per_dev * width
    return out.reshape(parts, side, side).astype(ml_dtypes.bfloat16)


def order_table(size, parts, per_dev):
    width = size // parts
    out = np.zeros((per_dev, size, parts, per_dev, width), np.float32)
    for p in range(per_dev):
        for y in range(size):
            out[p, y, y % parts, p, y // parts] = 1.0
    return out.reshape(per_dev * size, parts * per_dev * width).astype(ml_dtypes.bfloat16)


def dot(a, b):
    return jnp.dot(a, b, preferred_element_type=F32)


def dot_nt(a, b):
    return lax.dot_general(a, b, (((1,), (1,)), ((), ())), preferred_element_type=F32)


def to_planes_kernel(c_ref, t_ref, o_ref, scr):
    half = t_ref.shape[0] // 2
    devices = half // 2
    rows = scr.shape[0] // devices
    blocks = rows // 2
    low = lax.broadcasted_iota(jnp.int32, (half, 128), 1) < 64
    for g in range(blocks // 4):
        r = dot_nt(t_ref[...], c_ref[g * 256 : (g + 1) * 256, :])
        for h in range(2):
            a = r[:half, h * 128 : (h + 1) * 128]
            b = r[half:, h * 128 : (h + 1) * 128]
            even = jnp.where(low, a, pltpu.roll(b, 64, 1))
            odd = jnp.where(low, pltpu.roll(a, 64, 1), b)
            for d in range(2):
                at = d * blocks + g * 4 + h * 2
                part = slice(d * devices, (d + 1) * devices)
                scr[pl.ds(at, devices, stride=rows), :] = even[part]
                scr[pl.ds(at + 1, devices, stride=rows), :] = odd[part]
    o_ref[...] = scr[...].astype(BF16)


def from_planes_kernel(count, x_ref, t_hbm, o_ref, m_ref, scr, table, sem):
    copy = pltpu.make_async_copy(t_hbm, table, sem)
    copy.start()
    devices = t_hbm.shape[0] // 4
    rows = scr.shape[0] // devices
    blocks = rows // 2 - 1
    bands = m_ref.shape[2]
    scr[...] = x_ref[...].astype(F32)
    line = jnp.sum(scr[pl.ds(2 * blocks, devices, stride=rows), :], axis=0, keepdims=True)
    width = 2 * bands
    total = line[:, :width] + (line[:, width : 2 * width] + line[:, 2 * width : 3 * width])
    total = total / count
    m_ref[0] = total[:, :bands]
    m_ref[1] = total[:, bands:]
    copy.wait()
    for g in range(blocks // 4):
        parts = []
        for m in range(g * 4, g * 4 + 4):
            y = jnp.concatenate(
                [scr[pl.ds(d * blocks + m, devices, stride=rows), :] for d in range(2)], axis=0
            )
            y = jnp.transpose(y).astype(BF16)
            parts.append(jnp.concatenate([y[:64], y[64:]], axis=1))
        left = jnp.concatenate(parts, axis=0)
        o_ref[g * 256 : (g + 1) * 256, :] = dot(left, table[...]).astype(BF16)


def prepare_kernel(
    row_ref, col_ref, v_ref, f_ref, b_ref, ord_ref, tx_hbm, xt_hbm, v4_hbm, tx, xt, v4, sems
):
    size = f_ref.shape[0] // 2
    count = row_ref.shape[1]

    def hot(code, iota, s, axis):
        turn = (s * ((code >> 1) & 3) + (code & 1)) & 3
        hit = iota == (code >> 3)
        real = jnp.where(turn == 0, 1.0, jnp.where(turn == 2, -1.0, 0.0))
        imag = jnp.where(turn == 1, 1.0, jnp.where(turn == 3, -1.0, 0.0))
        return jnp.concatenate(
            [jnp.where(hit, real, 0.0), jnp.where(hit, imag, 0.0)], axis=axis
        ).astype(BF16)

    copies = []
    rows = lax.broadcasted_iota(jnp.int32, (size, count), 0)
    cols = lax.broadcasted_iota(jnp.int32, (count, size), 1)
    for s in range(4):
        part = slice(s * 2 * size, (s + 1) * 2 * size)
        tx[part, :] = dot(b_ref[...], hot(row_ref[...], rows, s, 0)).astype(BF16)
        copies.append(pltpu.make_async_copy(tx.at[part], tx_hbm.at[part], sems.at[s]))
        copies[-1].start()
        xt[:, part] = dot(hot(col_ref[...], cols, s, 1), f_ref[...]).astype(BF16)
    copies.append(pltpu.make_async_copy(xt, xt_hbm, sems.at[4]))
    copies[-1].start()
    v = jnp.concatenate([v_ref[0], v_ref[1]], axis=1)
    high = v.astype(BF16)
    rest = (v - high.astype(F32)).astype(BF16)
    both = dot(high, ord_ref[...]) + dot(rest, ord_ref[...])
    for s in range(4):
        v4[s] = both[:, s * 128 : (s + 1) * 128]
    copies.append(pltpu.make_async_copy(v4, v4_hbm, sems.at[5]))
    copies[-1].start()
    for copy in copies:
        copy.wait()


def planes_kernel(
    groups, r_ref, tx_hbm, xt_hbm, v4_hbm, yf_ref, yb_ref, o_ref,
    tx, xt, v4, h, r_scr, p_scr, left_scr, right_scr, sems,
):
    size = v4.shape[1]
    bands, count = r_ref.shape[0], r_ref.shape[1]
    ffts = sum(groups)
    rows, blocks = count // ffts, count // ffts // 2
    message = o_ref.shape[0] // (bands * ffts)
    pitch = p_scr.shape[0] // bands
    width = 2 * bands
    load_v = pltpu.make_async_copy(v4_hbm, v4, sems.at[5])
    loads = []
    for s in range(4):
        part = slice(s * 2 * size, (s + 1) * 2 * size)
        loads.append(pltpu.make_async_copy(tx_hbm.at[part], tx.at[part], sems.at[s]))
    load_xt = pltpu.make_async_copy(xt_hbm, xt, sems.at[4])
    loads[0].start()
    load_v.start()
    for copy in loads[1:]:
        copy.start()
    load_xt.start()
    for b in range(bands):
        r_scr[b * count : (b + 1) * count, :] = r_ref[b].astype(F32)

    def side(scr, start, stride):
        tiles = []
        for m in range(blocks):
            real = scr[pl.ds(start + m, bands, stride=stride), :]
            imag = scr[pl.ds(start + blocks + m, bands, stride=stride), :]
            tiles.append(jnp.concatenate([real, imag], axis=0).astype(BF16))
        return jnp.concatenate(tiles, axis=1)

    for s in range(4):
        loads[s].wait()
        w = jnp.concatenate([r_ref[b] for b in range(bands)], axis=1)
        g = dot(tx[s * 2 * size : (s + 1) * 2 * size, :], w).astype(BF16)
        left = jnp.concatenate(
            [
                jnp.concatenate(
                    [g[:size, b * 128 : (b + 1) * 128], g[size:, b * 128 : (b + 1) * 128]], axis=1
                )
                for b in range(bands)
            ],
            axis=0,
        )
        if s == 0:
            load_v.wait()
        for f in range(s * ffts // 4, (s + 1) * ffts // 4):
            left_scr[f * width : (f + 1) * width, :] = side(r_scr, f * rows, count)
        v = jnp.concatenate([v4[s], v4[s]], axis=1)
        field = (dot(left, yf_ref[s]) * jnp.concatenate([v] * bands, axis=0)).astype(BF16)
        back = dot(field, yb_ref[s]).astype(BF16)
        row = s * 2 * size
        for b in range(bands):
            part = back[b * size : (b + 1) * size]
            h[row : row + size, b * 128 : (b + 1) * 128] = part[:, :128]
            h[row + size : row + 2 * size, b * 128 : (b + 1) * 128] = part[:, 128:]

    load_xt.wait()
    ready = []

    def pack(f):
        right_scr[f * width : (f + 1) * width, :] = side(p_scr, f * message, pitch)

    def products(sources):
        part = slice(sources[0] * width, (sources[-1] + 1) * width)
        square = dot_nt(left_scr[part, :], right_scr[part, :])
        block = lax.broadcasted_iota(jnp.int32, square.shape, 0) // width
        same = block == lax.broadcasted_iota(jnp.int32, square.shape, 1) // width
        square = jnp.where(same, square, 0.0)
        total = sum(square[f * width : (f + 1) * width] for f in range(len(sources)))
        return jnp.concatenate([total, jnp.zeros((width, 128 - total.shape[1]), F32)], axis=1)

    gram = jnp.zeros((width, 128), F32)
    first = 0
    for group in groups:
        for n in range(bands // 2):
            if n < 2:
                for f in ready[n::2]:
                    pack(f)
            if n == 2 and ready:
                gram = gram + products(ready)
            out = dot(xt[first * rows : (first + group) * rows, :], h[:, n * 256 : (n + 1) * 256])
            for f in range(group):
                for j in range(2):
                    at = (2 * n + j) * pitch + (first + f) * message
                    part = out[f * rows : (f + 1) * rows, j * 128 : (j + 1) * 128]
                    p_scr[at : at + rows, :] = part
        ready = list(range(first, first + group))
        first += group
    for f in ready:
        pack(f)
    band = ffts * message
    for b in range(bands):
        o_ref[b * band : (b + 1) * band, :] = p_scr[b * pitch : b * pitch + band, :].astype(BF16)
    gram = gram + products(ready)
    for shift in (64, 32, 16):
        gram = gram + pltpu.roll(gram, shift, 1)
    lane = lax.broadcasted_iota(jnp.int32, (bands, 128), 1)
    turned = pltpu.roll(gram[bands:], bands, 1)
    total = gram[:bands] + jnp.where(lane % width < bands, turned, -turned)
    high = total.astype(BF16).astype(F32)
    middle = (total - high).astype(BF16).astype(F32)
    low = total - high - middle
    lines = jnp.where(lane < width, high, jnp.where(lane < 2 * width, middle, low))
    lines = jnp.where(lane < 3 * width, lines, 0.0)
    for b in range(bands):
        part = jnp.broadcast_to(lines[b : b + 1], (message - rows, 128)).astype(BF16)
        for f in range(ffts):
            at = (b * ffts + f) * message + rows
            o_ref[at : at + message - rows, :] = part


def call(kernel, out_shape, scratch, flops, args, in_hbm=(), out_hbm=False, limit=40):
    read = sum(a.size * a.dtype.itemsize for a in args)
    outs = jax.tree.leaves(out_shape, is_leaf=lambda s: hasattr(s, "shape"))
    written = sum(math.prod(s.shape) * jnp.dtype(s.dtype).itemsize for s in outs)
    args = [
        pltpu.with_memory_space_constraint(a, pltpu.HBM) if i in in_hbm else a
        for i, a in enumerate(args)
    ]
    return pl.pallas_call(
        kernel,
        out_shape=out_shape,
        in_specs=[HBM if i in in_hbm else VMEM for i in range(len(args))],
        out_specs=[HBM if out_hbm else VMEM] * len(outs) if isinstance(out_shape, tuple) else VMEM,
        scratch_shapes=scratch,
        compiler_params=pltpu.CompilerParams(vmem_limit_bytes=limit * 2**20),
        cost_estimate=pl.CostEstimate(flops=flops, bytes_accessed=read + written, transcendentals=0),
    )(*args)


def body(coeffs, potential, pattern):
    block_count, block_width = coeffs.shape[1], coeffs.shape[2]
    size = coeffs.shape[-1]
    bands, ffts = lax.axis_size("band"), lax.axis_size("fft")
    devices = bands * ffts
    per_dev = size // devices
    sticks = block_count * block_width
    rows = 2 * block_count
    shape = jax.ShapeDtypeStruct

    table = jnp.asarray(plane_table(size, bands, ffts))
    forward = dft_table(size, 1.0).reshape(2 * size, 2 * size)
    y_forward = split_table(size, 4, per_dev)
    y_backward = np.ascontiguousarray(y_forward.transpose(0, 2, 1))

    sent = call(
        to_planes_kernel,
        shape((devices * rows, 128), BF16),
        [pltpu.VMEM((devices * rows, 128), F32)],
        2 * sticks * (2 * size) ** 2,
        (coeffs.reshape(sticks, 2 * size), table),
    )
    got = lax.all_to_all(
        sent.reshape(devices, rows, 128), AXES, split_axis=0, concat_axis=0, tiled=True
    )
    got = got.reshape(bands, ffts * rows, 128)

    order = pattern.reshape(ffts, 1, block_count) * 2 + jnp.arange(2, dtype=jnp.int32)[None, :, None]
    planes = lax.dynamic_slice_in_dim(potential, lax.axis_index("band") * per_dev, per_dev, 0)
    count = ffts * rows
    tables = (
        pltpu.HBM((8 * size, count), BF16),
        pltpu.HBM((count, 8 * size), BF16),
        pltpu.HBM((4, size, per_dev * size // 4), F32),
    )
    held = [pltpu.VMEM(t.shape, t.dtype) for t in tables]
    x_table, x_back, v4 = call(
        prepare_kernel,
        tables,
        held + [pltpu.SemaphoreType.DMA((6,))],
        2 * 2 * 4 * count * (2 * size) ** 2,
        (
            order.reshape(1, count),
            order.reshape(count, 1),
            planes,
            jnp.asarray(forward),
            jnp.asarray(np.ascontiguousarray(forward.T)),
            jnp.asarray(order_table(size, 4, per_dev)),
        ),
        out_hbm=True,
    )

    message = rows + 2
    picked = call(
        functools.partial(planes_kernel, (6, 6, 4)),
        shape((devices * message, 128), BF16),
        held
        + [
            pltpu.VMEM((8 * size, bands * 128), BF16),
            pltpu.VMEM((bands * count, 128), F32),
            pltpu.VMEM((devices * message + 8 * bands, 128), F32),
            pltpu.VMEM((ffts * 2 * bands, block_count * 128), BF16),
            pltpu.VMEM((ffts * 2 * bands, block_count * 128), BF16),
            pltpu.SemaphoreType.DMA((6,)),
        ],
        2 * bands * 128 * 2 * 8 * size * count,
        (got, x_table, x_back, v4, jnp.asarray(y_forward), jnp.asarray(y_backward)),
        in_hbm=(1, 2, 3),
    )
    returned = lax.all_to_all(
        picked.reshape(devices, message // 2, 2, 128), AXES, split_axis=0, concat_axis=0, tiled=True
    )

    total_count = block_count * ffts * block_width * size
    images, matrix_rows = call(
        functools.partial(from_planes_kernel, total_count),
        (shape((sticks, 2 * size), BF16), shape((2, 1, bands), F32)),
        [
            pltpu.VMEM((devices * message, 128), F32),
            pltpu.VMEM((2 * size, 2 * size), BF16),
            pltpu.SemaphoreType.DMA(()),
        ],
        2 * sticks * (2 * size) ** 2,
        (returned.reshape(devices * message, 128), table),
        in_hbm=(1,),
    )
    return (images.reshape(coeffs.shape), matrix_rows)


def solution(mesh):
    placed = (P("band", "fft", None, None, None), P("fft", None, None), P())
    return jax.shard_map(
        body,
        mesh=mesh,
        in_specs=placed,
        out_specs=(P("band", "fft", None, None, None), P(None, "band", None)),
        check_vma=False,
    )
```

```python
import functools
import math

import jax
import jax.numpy as jnp
import ml_dtypes
import numpy as np
from jax import lax
from jax.experimental import pallas as pl
from jax.experimental.pallas import tpu as pltpu
from jax.sharding import PartitionSpec as P

F32 = jnp.float32
BF16 = jnp.bfloat16
AXES = ("band", "fft")
VMEM = pl.BlockSpec(memory_space=pltpu.VMEM)
HBM = pl.BlockSpec(memory_space=pltpu.HBM)


def dft_table(size, sign):
    counter = np.arange(size)
    angles = (counter[:, None] * counter[None, :] % size) * (2.0 * math.pi / size)
    cosine = np.cos(angles) / math.sqrt(size)
    sine = sign * np.sin(angles) / math.sqrt(size)
    table = np.stack([np.stack([cosine, sine], 1), np.stack([-sine, cosine], 1)], 0)
    return table.astype(ml_dtypes.bfloat16)


def plane_table(size, bands, ffts):
    per_fft = size // ffts
    per_dev = per_fft // bands
    forward = dft_table(size, 1.0)
    p, b, f = np.meshgrid(np.arange(per_dev), np.arange(bands), np.arange(ffts), indexing="ij")
    z = (f * per_fft + b * per_dev + p).reshape(-1)
    rows = forward[:, :, :, z].reshape(2, size, 2, per_dev, bands * ffts)
    return np.ascontiguousarray(rows.transpose(3, 2, 4, 0, 1)).reshape(2 * size, 2 * size)


def split_table(size, parts, per_dev):
    width = size // parts
    forward = dft_table(size, 1.0).astype(np.float32)
    out = np.zeros((parts, 2, per_dev, width, 2, per_dev, width), np.float32)
    for s in range(parts):
        part = forward[:, :width, :, s::parts]
        for p in range(per_dev):
            out[s, :, p, :, :, p, :] = part
    side = 2 * per_dev * width
    return out.reshape(parts, side, side).astype(ml_dtypes.bfloat16)


def order_table(size, parts, per_dev):
    width = size // parts
    out = np.zeros((per_dev, size, parts, per_dev, width), np.float32)
    for p in range(per_dev):
        for y in range(size):
            out[p, y, y % parts, p, y // parts] = 1.0
    return out.reshape(per_dev * size, parts * per_dev * width).astype(ml_dtypes.bfloat16)


def dot(a, b):
    return jnp.dot(a, b, preferred_element_type=F32)


def dot_nt(a, b):
    return lax.dot_general(a, b, (((1,), (1,)), ((), ())), preferred_element_type=F32)


def to_planes_kernel(c_ref, t_ref, o_ref, scr):
    half = t_ref.shape[1] // 2
    devices = half // 2
    rows = scr.shape[0] // devices
    blocks = rows // 2
    for g in range(blocks // 4):
        r = dot(c_ref[g * 256 : (g + 1) * 256, :], t_ref[...])
        for i in range(4):
            part = r[i * 64 : (i + 1) * 64]
            part = jnp.transpose(jnp.concatenate([part[:, :half], part[:, half:]], axis=0))
            for d in range(2):
                at = pl.ds(d * blocks + g * 4 + i, devices, stride=rows)
                scr[at, :] = part[d * devices : (d + 1) * devices]
    o_ref[...] = scr[...].astype(BF16)


def from_planes_kernel(count, x_ref, t_ref, o_ref, m_ref, scr):
    devices = t_ref.shape[0] // 4
    rows = scr.shape[0] // devices
    blocks = rows // 2 - 1
    bands = m_ref.shape[2]
    scr[...] = x_ref[...].astype(F32)
    line = jnp.sum(scr[pl.ds(2 * blocks, devices, stride=rows), :], axis=0, keepdims=True)
    width = 2 * bands
    total = line[:, :width] + (line[:, width : 2 * width] + line[:, 2 * width : 3 * width])
    total = total / count
    m_ref[0] = total[:, :bands]
    m_ref[1] = total[:, bands:]
    for g in range(blocks // 4):
        parts = []
        for m in range(g * 4, g * 4 + 4):
            y = jnp.concatenate(
                [scr[pl.ds(d * blocks + m, devices, stride=rows), :] for d in range(2)], axis=0
            )
            y = jnp.transpose(y).astype(BF16)
            parts.append(jnp.concatenate([y[:64], y[64:]], axis=1))
        left = jnp.concatenate(parts, axis=0)
        o_ref[g * 256 : (g + 1) * 256, :] = dot(left, t_ref[...]).astype(BF16)


def prepare_kernel(
    row_ref, col_ref, v_ref, f_ref, b_ref, ord_ref, tx_hbm, xt_hbm, v4_hbm, tx, xt, v4, sems
):
    size = f_ref.shape[0] // 2
    count = row_ref.shape[1]

    def hot(code, iota, s, axis):
        turn = (s * ((code >> 1) & 3) + (code & 1)) & 3
        hit = iota == (code >> 3)
        real = jnp.where(turn == 0, 1.0, jnp.where(turn == 2, -1.0, 0.0))
        imag = jnp.where(turn == 1, 1.0, jnp.where(turn == 3, -1.0, 0.0))
        return jnp.concatenate(
            [jnp.where(hit, real, 0.0), jnp.where(hit, imag, 0.0)], axis=axis
        ).astype(BF16)

    copies = []
    rows = lax.broadcasted_iota(jnp.int32, (size, count), 0)
    cols = lax.broadcasted_iota(jnp.int32, (count, size), 1)
    for s in range(4):
        part = slice(s * 2 * size, (s + 1) * 2 * size)
        tx[part, :] = dot(b_ref[...], hot(row_ref[...], rows, s, 0)).astype(BF16)
        copies.append(pltpu.make_async_copy(tx.at[part], tx_hbm.at[part], sems.at[s]))
        copies[-1].start()
        xt[:, part] = dot(hot(col_ref[...], cols, s, 1), f_ref[...]).astype(BF16)
    copies.append(pltpu.make_async_copy(xt, xt_hbm, sems.at[4]))
    copies[-1].start()
    v = jnp.concatenate([v_ref[0], v_ref[1]], axis=1)
    high = v.astype(BF16)
    rest = (v - high.astype(F32)).astype(BF16)
    both = dot(high, ord_ref[...]) + dot(rest, ord_ref[...])
    for s in range(4):
        v4[s] = both[:, s * 128 : (s + 1) * 128]
    copies.append(pltpu.make_async_copy(v4, v4_hbm, sems.at[5]))
    copies[-1].start()
    for copy in copies:
        copy.wait()


def planes_kernel(
    groups, r_ref, tx_hbm, xt_hbm, v4_hbm, yf_ref, yb_ref, o_ref,
    tx, xt, v4, h, r_scr, p_scr, left_scr, right_scr, sems,
):
    size = v4.shape[1]
    bands, count = r_ref.shape[0], r_ref.shape[1]
    ffts = sum(groups)
    rows, blocks = count // ffts, count // ffts // 2
    message = o_ref.shape[0] // (bands * ffts)
    pitch = p_scr.shape[0] // bands
    width = 2 * bands
    load_v = pltpu.make_async_copy(v4_hbm, v4, sems.at[5])
    loads = []
    for s in range(4):
        part = slice(s * 2 * size, (s + 1) * 2 * size)
        loads.append(pltpu.make_async_copy(tx_hbm.at[part], tx.at[part], sems.at[s]))
    load_xt = pltpu.make_async_copy(xt_hbm, xt, sems.at[4])
    loads[0].start()
    load_v.start()
    for copy in loads[1:]:
        copy.start()
    load_xt.start()
    for b in range(bands):
        r_scr[b * count : (b + 1) * count, :] = r_ref[b].astype(F32)

    def side(scr, start, stride):
        tiles = []
        for m in range(blocks):
            real = scr[pl.ds(start + m, bands, stride=stride), :]
            imag = scr[pl.ds(start + blocks + m, bands, stride=stride), :]
            tiles.append(jnp.concatenate([real, imag], axis=0).astype(BF16))
        return jnp.concatenate(tiles, axis=1)

    for s in range(4):
        loads[s].wait()
        w = jnp.concatenate([r_ref[b] for b in range(bands)], axis=1)
        g = dot(tx[s * 2 * size : (s + 1) * 2 * size, :], w).astype(BF16)
        left = jnp.concatenate(
            [
                jnp.concatenate(
                    [g[:size, b * 128 : (b + 1) * 128], g[size:, b * 128 : (b + 1) * 128]], axis=1
                )
                for b in range(bands)
            ],
            axis=0,
        )
        if s == 0:
            load_v.wait()
        for f in range(s * ffts // 4, (s + 1) * ffts // 4):
            left_scr[f * width : (f + 1) * width, :] = side(r_scr, f * rows, count)
        v = jnp.concatenate([v4[s], v4[s]], axis=1)
        field = (dot(left, yf_ref[s]) * jnp.concatenate([v] * bands, axis=0)).astype(BF16)
        back = dot(field, yb_ref[s]).astype(BF16)
        row = s * 2 * size
        for b in range(bands):
            part = back[b * size : (b + 1) * size]
            h[row : row + size, b * 128 : (b + 1) * 128] = part[:, :128]
            h[row + size : row + 2 * size, b * 128 : (b + 1) * 128] = part[:, 128:]

    load_xt.wait()
    ready = []

    def pack(f):
        right_scr[f * width : (f + 1) * width, :] = side(p_scr, f * message, pitch)

    def products(sources):
        part = slice(sources[0] * width, (sources[-1] + 1) * width)
        square = dot_nt(left_scr[part, :], right_scr[part, :])
        block = lax.broadcasted_iota(jnp.int32, square.shape, 0) // width
        same = block == lax.broadcasted_iota(jnp.int32, square.shape, 1) // width
        square = jnp.where(same, square, 0.0)
        total = sum(square[f * width : (f + 1) * width] for f in range(len(sources)))
        return jnp.concatenate([total, jnp.zeros((width, 128 - total.shape[1]), F32)], axis=1)

    gram = jnp.zeros((width, 128), F32)
    first = 0
    for group in groups:
        for n in range(bands // 2):
            if n < 2:
                for f in ready[n::2]:
                    pack(f)
            if n == 2 and ready:
                gram = gram + products(ready)
            out = dot(xt[first * rows : (first + group) * rows, :], h[:, n * 256 : (n + 1) * 256])
            for f in range(group):
                for j in range(2):
                    at = (2 * n + j) * pitch + (first + f) * message
                    part = out[f * rows : (f + 1) * rows, j * 128 : (j + 1) * 128]
                    p_scr[at : at + rows, :] = part
        ready = list(range(first, first + group))
        first += group
    for f in ready:
        pack(f)
    band = ffts * message
    for b in range(bands):
        o_ref[b * band : (b + 1) * band, :] = p_scr[b * pitch : b * pitch + band, :].astype(BF16)
    gram = gram + products(ready)
    for shift in (64, 32, 16):
        gram = gram + pltpu.roll(gram, shift, 1)
    lane = lax.broadcasted_iota(jnp.int32, (bands, 128), 1)
    turned = pltpu.roll(gram[bands:], bands, 1)
    total = gram[:bands] + jnp.where(lane % width < bands, turned, -turned)
    high = total.astype(BF16).astype(F32)
    middle = (total - high).astype(BF16).astype(F32)
    low = total - high - middle
    lines = jnp.where(lane < width, high, jnp.where(lane < 2 * width, middle, low))
    lines = jnp.where(lane < 3 * width, lines, 0.0)
    for b in range(bands):
        part = jnp.broadcast_to(lines[b : b + 1], (message - rows, 128)).astype(BF16)
        for f in range(ffts):
            at = (b * ffts + f) * message + rows
            o_ref[at : at + message - rows, :] = part


def call(kernel, out_shape, scratch, flops, args, in_hbm=(), out_hbm=False, limit=40):
    read = sum(a.size * a.dtype.itemsize for a in args)
    outs = jax.tree.leaves(out_shape, is_leaf=lambda s: hasattr(s, "shape"))
    written = sum(math.prod(s.shape) * jnp.dtype(s.dtype).itemsize for s in outs)
    args = [
        pltpu.with_memory_space_constraint(a, pltpu.HBM) if i in in_hbm else a
        for i, a in enumerate(args)
    ]
    return pl.pallas_call(
        kernel,
        out_shape=out_shape,
        in_specs=[HBM if i in in_hbm else VMEM for i in range(len(args))],
        out_specs=[HBM if out_hbm else VMEM] * len(outs) if isinstance(out_shape, tuple) else VMEM,
        scratch_shapes=scratch,
        compiler_params=pltpu.CompilerParams(vmem_limit_bytes=limit * 2**20),
        cost_estimate=pl.CostEstimate(flops=flops, bytes_accessed=read + written, transcendentals=0),
    )(*args)


def body(coeffs, potential, pattern):
    block_count, block_width = coeffs.shape[1], coeffs.shape[2]
    size = coeffs.shape[-1]
    bands, ffts = lax.axis_size("band"), lax.axis_size("fft")
    devices = bands * ffts
    per_dev = size // devices
    sticks = block_count * block_width
    rows = 2 * block_count
    shape = jax.ShapeDtypeStruct

    table = plane_table(size, bands, ffts)
    forward = dft_table(size, 1.0).reshape(2 * size, 2 * size)
    y_forward = split_table(size, 4, per_dev)
    y_backward = np.ascontiguousarray(y_forward.transpose(0, 2, 1))

    sent = call(
        to_planes_kernel,
        shape((devices * rows, 128), BF16),
        [pltpu.VMEM((devices * rows, 128), F32)],
        2 * sticks * (2 * size) ** 2,
        (coeffs.reshape(sticks, 2 * size), jnp.asarray(np.ascontiguousarray(table.T))),
    )
    got = lax.all_to_all(
        sent.reshape(devices, rows, 128), AXES, split_axis=0, concat_axis=0, tiled=True
    )
    got = got.reshape(bands, ffts * rows, 128)

    order = pattern.reshape(ffts, 1, block_count) * 2 + jnp.arange(2, dtype=jnp.int32)[None, :, None]
    planes = lax.dynamic_slice_in_dim(potential, lax.axis_index("band") * per_dev, per_dev, 0)
    count = ffts * rows
    tables = (
        pltpu.HBM((8 * size, count), BF16),
        pltpu.HBM((count, 8 * size), BF16),
        pltpu.HBM((4, size, per_dev * size // 4), F32),
    )
    held = [pltpu.VMEM(t.shape, t.dtype) for t in tables]
    x_table, x_back, v4 = call(
        prepare_kernel,
        tables,
        held + [pltpu.SemaphoreType.DMA((6,))],
        2 * 2 * 4 * count * (2 * size) ** 2,
        (
            order.reshape(1, count),
            order.reshape(count, 1),
            planes,
            jnp.asarray(forward),
            jnp.asarray(np.ascontiguousarray(forward.T)),
            jnp.asarray(order_table(size, 4, per_dev)),
        ),
        out_hbm=True,
    )

    message = rows + 2
    picked = call(
        functools.partial(planes_kernel, (6, 6, 4)),
        shape((devices * message, 128), BF16),
        held
        + [
            pltpu.VMEM((8 * size, bands * 128), BF16),
            pltpu.VMEM((bands * count, 128), F32),
            pltpu.VMEM((devices * message + 8 * bands, 128), F32),
            pltpu.VMEM((ffts * 2 * bands, block_count * 128), BF16),
            pltpu.VMEM((ffts * 2 * bands, block_count * 128), BF16),
            pltpu.SemaphoreType.DMA((6,)),
        ],
        2 * bands * 128 * 2 * 8 * size * count,
        (got, x_table, x_back, v4, jnp.asarray(y_forward), jnp.asarray(y_backward)),
        in_hbm=(1, 2, 3),
    )
    returned = lax.all_to_all(
        picked.reshape(devices, message // 2, 2, 128), AXES, split_axis=0, concat_axis=0, tiled=True
    )

    total_count = block_count * ffts * block_width * size
    images, matrix_rows = call(
        functools.partial(from_planes_kernel, total_count),
        (shape((sticks, 2 * size), BF16), shape((2, 1, bands), F32)),
        [pltpu.VMEM((devices * message, 128), F32)],
        2 * sticks * (2 * size) ** 2,
        (returned.reshape(devices * message, 128), jnp.asarray(table)),
    )
    return (images.reshape(coeffs.shape), matrix_rows)


def solution(mesh):
    placed = (P("band", "fft", None, None, None), P("fft", None, None), P())
    return jax.shard_map(
        body,
        mesh=mesh,
        in_specs=placed,
        out_specs=(P("band", "fft", None, None, None), P(None, "band", None)),
        check_vma=False,
    )
```

```python
import functools
import math

import jax
import jax.numpy as jnp
import ml_dtypes
import numpy as np
from jax import lax
from jax.experimental import pallas as pl
from jax.experimental.pallas import tpu as pltpu
from jax.sharding import PartitionSpec as P

F32 = jnp.float32
BF16 = jnp.bfloat16
AXES = ("band", "fft")
VMEM = pl.BlockSpec(memory_space=pltpu.VMEM)
HBM = pl.BlockSpec(memory_space=pltpu.HBM)


def dft_table(size, sign):
    counter = np.arange(size)
    angles = (counter[:, None] * counter[None, :] % size) * (2.0 * math.pi / size)
    cosine = np.cos(angles) / math.sqrt(size)
    sine = sign * np.sin(angles) / math.sqrt(size)
    table = np.stack([np.stack([cosine, sine], 1), np.stack([-sine, cosine], 1)], 0)
    return table.astype(ml_dtypes.bfloat16)


def plane_table(size, bands, ffts):
    per_fft = size // ffts
    per_dev = per_fft // bands
    forward = dft_table(size, 1.0)
    p, b, f = np.meshgrid(np.arange(per_dev), np.arange(bands), np.arange(ffts), indexing="ij")
    z = (f * per_fft + b * per_dev + p).reshape(-1)
    rows = forward[:, :, :, z].reshape(2, size, 2, per_dev, bands * ffts)
    return np.ascontiguousarray(rows.transpose(3, 2, 4, 0, 1)).reshape(2 * size, 2 * size)


def split_table(size, parts, per_dev):
    width = size // parts
    forward = dft_table(size, 1.0).astype(np.float32)
    out = np.zeros((parts, 2, per_dev, width, 2, per_dev, width), np.float32)
    for s in range(parts):
        part = forward[:, :width, :, s::parts]
        for p in range(per_dev):
            out[s, :, p, :, :, p, :] = part
    side = 2 * per_dev * width
    return out.reshape(parts, side, side).astype(ml_dtypes.bfloat16)


def order_table(size, parts, per_dev):
    width = size // parts
    out = np.zeros((per_dev, size, parts, per_dev, width), np.float32)
    for p in range(per_dev):
        for y in range(size):
            out[p, y, y % parts, p, y // parts] = 1.0
    return out.reshape(per_dev * size, parts * per_dev * width).astype(ml_dtypes.bfloat16)


def dot(a, b):
    return jnp.dot(a, b, preferred_element_type=F32)


def dot_nt(a, b):
    return lax.dot_general(a, b, (((1,), (1,)), ((), ())), preferred_element_type=F32)


def to_planes_kernel(c_ref, t_ref, o_ref, scr):
    half = t_ref.shape[1] // 2
    devices = half // 2
    rows = scr.shape[0] // devices
    blocks = rows // 2
    for g in range(blocks // 4):
        r = dot(c_ref[g * 256 : (g + 1) * 256, :], t_ref[...])
        for i in range(4):
            part = r[i * 64 : (i + 1) * 64]
            part = jnp.transpose(jnp.concatenate([part[:, :half], part[:, half:]], axis=0))
            for d in range(2):
                at = pl.ds(d * blocks + g * 4 + i, devices, stride=rows)
                scr[at, :] = part[d * devices : (d + 1) * devices]
    o_ref[...] = scr[...].astype(BF16)


def from_planes_kernel(count, x_ref, t_ref, o_hbm, m_ref, scr, out, low, high, sems):
    devices = t_ref.shape[0] // 4
    rows = scr.shape[0] // devices
    blocks = rows // 2 - 1
    bands = m_ref.shape[2]
    scr[...] = x_ref[...].astype(F32)
    line = jnp.sum(scr[pl.ds(2 * blocks, devices, stride=rows), :], axis=0, keepdims=True)
    width = 2 * bands
    total = line[:, :width] + (line[:, width : 2 * width] + line[:, 2 * width : 3 * width])
    total = total / count
    m_ref[0] = total[:, :bands]
    m_ref[1] = total[:, bands:]
    copies = []
    for g in range(blocks // 4):
        parts = []
        for m in range(g * 4, g * 4 + 4):
            y = jnp.concatenate(
                [scr[pl.ds(d * blocks + m, devices, stride=rows), :] for d in range(2)], axis=0
            )
            y = jnp.transpose(y).astype(BF16)
            parts.append(jnp.concatenate([y[:64], y[64:]], axis=1))
        value = dot(jnp.concatenate(parts, axis=0), t_ref[...])
        for half, lanes in ((low, 0), (high, 128)):
            for d in range(2):
                at = d * 256 + lanes
                half[g % 2, pl.ds(d, 256, stride=2), :] = value[:, at : at + 128]
        pairs = jnp.concatenate([low[g % 2], high[g % 2]], axis=1).astype(BF16)
        out[g * 256 : (g + 1) * 256] = pairs.reshape(256, 2, 256)
        part = pl.ds(g * 256, 256)
        copies.append(pltpu.make_async_copy(out.at[part], o_hbm.at[part], sems.at[g]))
        copies[-1].start()
    for copy in copies:
        copy.wait()


def prepare_kernel(
    row_ref, col_ref, v_ref, f_ref, b_ref, ord_ref, tx_hbm, xt_hbm, v4_hbm, tx, xt, v4, sems
):
    size = f_ref.shape[0] // 2
    count = row_ref.shape[1]

    def hot(code, iota, s, axis):
        turn = (s * ((code >> 1) & 3) + (code & 1)) & 3
        hit = iota == (code >> 3)
        real = jnp.where(turn == 0, 1.0, jnp.where(turn == 2, -1.0, 0.0))
        imag = jnp.where(turn == 1, 1.0, jnp.where(turn == 3, -1.0, 0.0))
        return jnp.concatenate(
            [jnp.where(hit, real, 0.0), jnp.where(hit, imag, 0.0)], axis=axis
        ).astype(BF16)

    copies = []
    rows = lax.broadcasted_iota(jnp.int32, (size, count), 0)
    cols = lax.broadcasted_iota(jnp.int32, (count, size), 1)
    for s in range(4):
        part = slice(s * 2 * size, (s + 1) * 2 * size)
        tx[part, :] = dot(b_ref[...], hot(row_ref[...], rows, s, 0)).astype(BF16)
        copies.append(pltpu.make_async_copy(tx.at[part], tx_hbm.at[part], sems.at[s]))
        copies[-1].start()
        xt[:, part] = dot(hot(col_ref[...], cols, s, 1), f_ref[...]).astype(BF16)
    copies.append(pltpu.make_async_copy(xt, xt_hbm, sems.at[4]))
    copies[-1].start()
    v = jnp.concatenate([v_ref[0], v_ref[1]], axis=1)
    high = v.astype(BF16)
    rest = (v - high.astype(F32)).astype(BF16)
    both = dot(high, ord_ref[...]) + dot(rest, ord_ref[...])
    for s in range(4):
        v4[s] = both[:, s * 128 : (s + 1) * 128]
    copies.append(pltpu.make_async_copy(v4, v4_hbm, sems.at[5]))
    copies[-1].start()
    for copy in copies:
        copy.wait()


def planes_kernel(
    groups, r_ref, tx_hbm, xt_hbm, v4_hbm, yf_hbm, yb_hbm, o_ref,
    tx, xt, v4, yf, yb, h, r_scr, p_scr, left_scr, right_scr, sems,
):
    size = v4.shape[1]
    bands, count = r_ref.shape[0], r_ref.shape[1]
    ffts = sum(groups)
    rows, blocks = count // ffts, count // ffts // 2
    message = o_ref.shape[0] // (bands * ffts)
    pitch = p_scr.shape[0] // bands
    width = 2 * bands
    load_v = pltpu.make_async_copy(v4_hbm, v4, sems.at[5])
    load_f = pltpu.make_async_copy(yf_hbm, yf, sems.at[6])
    load_b = pltpu.make_async_copy(yb_hbm, yb, sems.at[7])
    loads = []
    for s in range(4):
        part = slice(s * 2 * size, (s + 1) * 2 * size)
        loads.append(pltpu.make_async_copy(tx_hbm.at[part], tx.at[part], sems.at[s]))
    load_xt = pltpu.make_async_copy(xt_hbm, xt, sems.at[4])
    loads[0].start()
    load_f.start()
    load_v.start()
    load_b.start()
    for copy in loads[1:]:
        copy.start()
    load_xt.start()
    for b in range(bands):
        r_scr[b * count : (b + 1) * count, :] = r_ref[b].astype(F32)

    def side(scr, start, stride):
        tiles = []
        for m in range(blocks):
            real = scr[pl.ds(start + m, bands, stride=stride), :]
            imag = scr[pl.ds(start + blocks + m, bands, stride=stride), :]
            tiles.append(jnp.concatenate([real, imag], axis=0).astype(BF16))
        return jnp.concatenate(tiles, axis=1)

    for s in range(4):
        loads[s].wait()
        w = jnp.concatenate([r_ref[b] for b in range(bands)], axis=1)
        g = dot(tx[s * 2 * size : (s + 1) * 2 * size, :], w).astype(BF16)
        left = jnp.concatenate(
            [
                jnp.concatenate(
                    [g[:size, b * 128 : (b + 1) * 128], g[size:, b * 128 : (b + 1) * 128]], axis=1
                )
                for b in range(bands)
            ],
            axis=0,
        )
        if s == 0:
            load_f.wait()
            load_v.wait()
            load_b.wait()
        for f in range(s * ffts // 4, (s + 1) * ffts // 4):
            left_scr[f * width : (f + 1) * width, :] = side(r_scr, f * rows, count)
        v = jnp.concatenate([v4[s], v4[s]], axis=1)
        field = (dot(left, yf[s]) * jnp.concatenate([v] * bands, axis=0)).astype(BF16)
        back = dot(field, yb[s]).astype(BF16)
        row = s * 2 * size
        for b in range(bands):
            part = back[b * size : (b + 1) * size]
            h[row : row + size, b * 128 : (b + 1) * 128] = part[:, :128]
            h[row + size : row + 2 * size, b * 128 : (b + 1) * 128] = part[:, 128:]

    load_xt.wait()
    ready = []

    def pack(f):
        right_scr[f * width : (f + 1) * width, :] = side(p_scr, f * message, pitch)

    def products(sources):
        part = slice(sources[0] * width, (sources[-1] + 1) * width)
        square = dot_nt(left_scr[part, :], right_scr[part, :])
        block = lax.broadcasted_iota(jnp.int32, square.shape, 0) // width
        same = block == lax.broadcasted_iota(jnp.int32, square.shape, 1) // width
        square = jnp.where(same, square, 0.0)
        total = sum(square[f * width : (f + 1) * width] for f in range(len(sources)))
        return jnp.concatenate([total, jnp.zeros((width, 128 - total.shape[1]), F32)], axis=1)

    gram = jnp.zeros((width, 128), F32)
    first = 0
    for group in groups:
        for n in range(bands // 2):
            if n < 2:
                for f in ready[n::2]:
                    pack(f)
            if n == 2 and ready:
                gram = gram + products(ready)
            out = dot(xt[first * rows : (first + group) * rows, :], h[:, n * 256 : (n + 1) * 256])
            for f in range(group):
                for j in range(2):
                    at = (2 * n + j) * pitch + (first + f) * message
                    part = out[f * rows : (f + 1) * rows, j * 128 : (j + 1) * 128]
                    p_scr[at : at + rows, :] = part
        ready = list(range(first, first + group))
        first += group
    for f in ready:
        pack(f)
    band = ffts * message
    for b in range(bands):
        o_ref[b * band : (b + 1) * band, :] = p_scr[b * pitch : b * pitch + band, :].astype(BF16)
    gram = gram + products(ready)
    for shift in (64, 32, 16):
        gram = gram + pltpu.roll(gram, shift, 1)
    lane = lax.broadcasted_iota(jnp.int32, (bands, 128), 1)
    turned = pltpu.roll(gram[bands:], bands, 1)
    total = gram[:bands] + jnp.where(lane % width < bands, turned, -turned)
    high = total.astype(BF16).astype(F32)
    middle = (total - high).astype(BF16).astype(F32)
    low = total - high - middle
    lines = jnp.where(lane < width, high, jnp.where(lane < 2 * width, middle, low))
    lines = jnp.where(lane < 3 * width, lines, 0.0)
    for b in range(bands):
        part = jnp.broadcast_to(lines[b : b + 1], (message - rows, 128)).astype(BF16)
        for f in range(ffts):
            at = (b * ffts + f) * message + rows
            o_ref[at : at + message - rows, :] = part


def call(kernel, out_shape, scratch, flops, args, in_hbm=(), out_hbm=(), limit=40):
    read = sum(a.size * a.dtype.itemsize for a in args)
    outs = out_shape if isinstance(out_shape, tuple) else (out_shape,)
    written = sum(math.prod(s.shape) * jnp.dtype(s.dtype).itemsize for s in outs)
    args = [
        pltpu.with_memory_space_constraint(a, pltpu.HBM) if i in in_hbm else a
        for i, a in enumerate(args)
    ]
    results = pl.pallas_call(
        kernel,
        out_shape=outs,
        in_specs=[HBM if i in in_hbm else VMEM for i in range(len(args))],
        out_specs=[HBM if i in out_hbm else VMEM for i in range(len(outs))],
        scratch_shapes=scratch,
        compiler_params=pltpu.CompilerParams(vmem_limit_bytes=limit * 2**20),
        cost_estimate=pl.CostEstimate(flops=flops, bytes_accessed=read + written, transcendentals=0),
    )(*args)
    return results if isinstance(out_shape, tuple) else results[0]


def body(coeffs, potential, pattern):
    block_count, block_width = coeffs.shape[1], coeffs.shape[2]
    size = coeffs.shape[-1]
    bands, ffts = lax.axis_size("band"), lax.axis_size("fft")
    devices = bands * ffts
    per_dev = size // devices
    sticks = block_count * block_width
    rows = 2 * block_count
    shape = jax.ShapeDtypeStruct

    table = plane_table(size, bands, ffts)
    forward = dft_table(size, 1.0).reshape(2 * size, 2 * size)
    y_forward = split_table(size, 4, per_dev)
    y_backward = np.ascontiguousarray(y_forward.transpose(0, 2, 1))

    sent = call(
        to_planes_kernel,
        pltpu.VMEM((devices * rows, 128), BF16),
        [pltpu.VMEM((devices * rows, 128), F32)],
        2 * sticks * (2 * size) ** 2,
        (coeffs.reshape(sticks, 2 * size), jnp.asarray(np.ascontiguousarray(table.T))),
    )
    got = lax.all_to_all(
        sent.reshape(devices, rows, 128), AXES, split_axis=0, concat_axis=0, tiled=True
    )
    got = got.reshape(bands, ffts * rows, 128)

    order = pattern.reshape(ffts, 1, block_count) * 2 + jnp.arange(2, dtype=jnp.int32)[None, :, None]
    planes = lax.dynamic_slice_in_dim(potential, lax.axis_index("band") * per_dev, per_dev, 0)
    count = ffts * rows
    tables = (
        pltpu.HBM((8 * size, count), BF16),
        pltpu.HBM((count, 8 * size), BF16),
        pltpu.HBM((4, size, per_dev * size // 4), F32),
    )
    held = [pltpu.VMEM(t.shape, t.dtype) for t in tables]
    x_table, x_back, v4 = call(
        prepare_kernel,
        tables,
        held + [pltpu.SemaphoreType.DMA((6,))],
        2 * 2 * 4 * count * (2 * size) ** 2,
        (
            order.reshape(1, count),
            order.reshape(count, 1),
            planes,
            jnp.asarray(forward),
            jnp.asarray(np.ascontiguousarray(forward.T)),
            jnp.asarray(order_table(size, 4, per_dev)),
        ),
        out_hbm=(0, 1, 2),
    )

    message = rows + 2
    picked = call(
        functools.partial(planes_kernel, (6, 6, 4)),
        shape((devices * message, 128), BF16),
        held
        + [
            pltpu.VMEM(y_forward.shape, BF16),
            pltpu.VMEM(y_forward.shape, BF16),
            pltpu.VMEM((8 * size, bands * 128), BF16),
            pltpu.VMEM((bands * count, 128), F32),
            pltpu.VMEM((devices * message + 8 * bands, 128), F32),
            pltpu.VMEM((ffts * 2 * bands, block_count * 128), BF16),
            pltpu.VMEM((ffts * 2 * bands, block_count * 128), BF16),
            pltpu.SemaphoreType.DMA((8,)),
        ],
        2 * bands * 128 * 2 * 8 * size * count,
        (got, x_table, x_back, v4, jnp.asarray(y_forward), jnp.asarray(y_backward)),
        in_hbm=(1, 2, 3, 4, 5),
    )
    returned = lax.all_to_all(
        picked.reshape(devices, message // 2, 2, 128), AXES, split_axis=0, concat_axis=0, tiled=True
    )

    total_count = block_count * ffts * block_width * size
    images, matrix_rows = call(
        functools.partial(from_planes_kernel, total_count),
        (pltpu.HBM((sticks, 2, size), BF16), shape((2, 1, bands), F32)),
        [
            pltpu.VMEM((devices * message, 128), F32),
            pltpu.VMEM((sticks, 2, size), BF16),
            pltpu.VMEM((2, 512, 128), F32),
            pltpu.VMEM((2, 512, 128), F32),
            pltpu.SemaphoreType.DMA((block_count // 4,)),
        ],
        2 * sticks * (2 * size) ** 2,
        (returned.reshape(devices * message, 128), jnp.asarray(table)),
        out_hbm=(0,),
    )
    return (images.reshape(coeffs.shape), matrix_rows)


def solution(mesh):
    placed = (P("band", "fft", None, None, None), P("fft", None, None), P())
    return jax.shard_map(
        body,
        mesh=mesh,
        in_specs=placed,
        out_specs=(P("band", "fft", None, None, None), P(None, "band", None)),
        check_vma=False,
    )
```

```python
import functools
import math

import jax
import jax.numpy as jnp
import ml_dtypes
import numpy as np
from jax import lax
from jax.experimental import pallas as pl
from jax.experimental.pallas import tpu as pltpu
from jax.sharding import PartitionSpec as P

F32 = jnp.float32
BF16 = jnp.bfloat16
AXES = ("band", "fft")
VMEM = pl.BlockSpec(memory_space=pltpu.VMEM)
HBM = pl.BlockSpec(memory_space=pltpu.HBM)


def dft_table(size, sign):
    counter = np.arange(size)
    angles = (counter[:, None] * counter[None, :] % size) * (2.0 * math.pi / size)
    cosine = np.cos(angles) / math.sqrt(size)
    sine = sign * np.sin(angles) / math.sqrt(size)
    table = np.stack([np.stack([cosine, sine], 1), np.stack([-sine, cosine], 1)], 0)
    return table.astype(ml_dtypes.bfloat16)


def plane_table(size, bands, ffts):
    per_fft = size // ffts
    per_dev = per_fft // bands
    forward = dft_table(size, 1.0)
    p, b, f = np.meshgrid(np.arange(per_dev), np.arange(bands), np.arange(ffts), indexing="ij")
    z = (f * per_fft + b * per_dev + p).reshape(-1)
    rows = forward[:, :, :, z].reshape(2, size, 2, per_dev, bands * ffts)
    return np.ascontiguousarray(rows.transpose(3, 2, 4, 0, 1)).reshape(2 * size, 2 * size)


def split_table(size, parts, per_dev):
    width = size // parts
    forward = dft_table(size, 1.0).astype(np.float32)
    out = np.zeros((parts, 2, per_dev, width, 2, per_dev, width), np.float32)
    for s in range(parts):
        part = forward[:, :width, :, s::parts]
        for p in range(per_dev):
            out[s, :, p, :, :, p, :] = part
    side = 2 * per_dev * width
    return out.reshape(parts, side, side).astype(ml_dtypes.bfloat16)


def order_table(size, parts, per_dev):
    width = size // parts
    out = np.zeros((per_dev, size, parts, per_dev, width), np.float32)
    for p in range(per_dev):
        for y in range(size):
            out[p, y, y % parts, p, y // parts] = 1.0
    return out.reshape(per_dev * size, parts * per_dev * width).astype(ml_dtypes.bfloat16)


def dot(a, b):
    return jnp.dot(a, b, preferred_element_type=F32)


def dot_nt(a, b):
    return lax.dot_general(a, b, (((1,), (1,)), ((), ())), preferred_element_type=F32)


def to_planes_kernel(c_ref, t_ref, o_ref, scr):
    half = t_ref.shape[1] // 2
    devices = half // 2
    rows = scr.shape[0] // devices
    blocks = rows // 2
    for g in range(blocks // 4):
        r = dot(c_ref[g * 256 : (g + 1) * 256, :], t_ref[...])
        for i in range(4):
            part = r[i * 64 : (i + 1) * 64]
            part = jnp.transpose(jnp.concatenate([part[:, :half], part[:, half:]], axis=0))
            for d in range(2):
                at = pl.ds(d * blocks + g * 4 + i, devices, stride=rows)
                scr[at, :] = part[d * devices : (d + 1) * devices]
    o_ref[...] = scr[...].astype(BF16)


def from_planes_kernel(count, x_ref, t_ref, o_hbm, m_ref, scr, out, low, high, sems):
    devices = t_ref.shape[0] // 4
    rows = scr.shape[0] // devices
    blocks = rows // 2 - 1
    bands = m_ref.shape[2]
    scr[...] = x_ref[...].astype(F32)
    total = sum(scr[pl.ds(2 * blocks + i, devices, stride=rows), :] for i in range(2))
    total = jnp.sum(total, axis=0, keepdims=True) / count
    m_ref[0] = total[:, :bands]
    m_ref[1] = total[:, bands : 2 * bands]
    copies = []
    for g in range(blocks // 4):
        parts = []
        for m in range(g * 4, g * 4 + 4):
            y = jnp.concatenate(
                [scr[pl.ds(d * blocks + m, devices, stride=rows), :] for d in range(2)], axis=0
            )
            y = jnp.transpose(y).astype(BF16)
            parts.append(jnp.concatenate([y[:64], y[64:]], axis=1))
        value = dot(jnp.concatenate(parts, axis=0), t_ref[...])
        for half, lanes in ((low, 0), (high, 128)):
            for d in range(2):
                at = d * 256 + lanes
                half[g % 2, pl.ds(d, 256, stride=2), :] = value[:, at : at + 128]
        pairs = jnp.concatenate([low[g % 2], high[g % 2]], axis=1).astype(BF16)
        out[g * 256 : (g + 1) * 256] = pairs.reshape(256, 2, 256)
        part = pl.ds(g * 256, 256)
        copies.append(pltpu.make_async_copy(out.at[part], o_hbm.at[part], sems.at[g]))
        copies[-1].start()
    for copy in copies:
        copy.wait()


def prepare_kernel(
    row_ref, col_ref, v_ref, f_ref, b_ref, ord_ref, tx_hbm, xt_hbm, v4_hbm, tx, xt, v4, sems
):
    size = f_ref.shape[0] // 2
    count = row_ref.shape[1]

    def hot(code, iota, s, axis):
        turn = (s * ((code >> 1) & 3) + (code & 1)) & 3
        hit = iota == (code >> 3)
        real = jnp.where(turn == 0, 1.0, jnp.where(turn == 2, -1.0, 0.0))
        imag = jnp.where(turn == 1, 1.0, jnp.where(turn == 3, -1.0, 0.0))
        return jnp.concatenate(
            [jnp.where(hit, real, 0.0), jnp.where(hit, imag, 0.0)], axis=axis
        ).astype(BF16)

    copies = []
    rows = lax.broadcasted_iota(jnp.int32, (size, count), 0)
    cols = lax.broadcasted_iota(jnp.int32, (count, size), 1)
    for s in range(4):
        part = slice(s * 2 * size, (s + 1) * 2 * size)
        tx[part, :] = dot(b_ref[...], hot(row_ref[...], rows, s, 0)).astype(BF16)
        copies.append(pltpu.make_async_copy(tx.at[part], tx_hbm.at[part], sems.at[s]))
        copies[-1].start()
        xt[:, part] = dot(hot(col_ref[...], cols, s, 1), f_ref[...]).astype(BF16)
    copies.append(pltpu.make_async_copy(xt, xt_hbm, sems.at[4]))
    copies[-1].start()
    v = jnp.concatenate([v_ref[0], v_ref[1]], axis=1)
    high = v.astype(BF16)
    rest = (v - high.astype(F32)).astype(BF16)
    both = dot(high, ord_ref[...]) + dot(rest, ord_ref[...])
    for s in range(4):
        v4[s] = both[:, s * 128 : (s + 1) * 128]
    copies.append(pltpu.make_async_copy(v4, v4_hbm, sems.at[5]))
    copies[-1].start()
    for copy in copies:
        copy.wait()


def planes_kernel(
    groups, r_ref, tx_hbm, xt_hbm, v4_hbm, yf_hbm, yb_hbm, o_ref,
    tx, xt, v4, yf, yb, h, r_scr, p_scr, sems,
):
    size = v4.shape[1]
    bands, count = r_ref.shape[0], r_ref.shape[1]
    ffts = sum(groups)
    rows, blocks = count // ffts, count // ffts // 2
    message = o_ref.shape[0] // (bands * ffts)
    load_v = pltpu.make_async_copy(v4_hbm, v4, sems.at[5])
    load_f = pltpu.make_async_copy(yf_hbm, yf, sems.at[6])
    load_b = pltpu.make_async_copy(yb_hbm, yb, sems.at[7])
    loads = []
    for s in range(4):
        part = slice(s * 2 * size, (s + 1) * 2 * size)
        loads.append(pltpu.make_async_copy(tx_hbm.at[part], tx.at[part], sems.at[s]))
    load_xt = pltpu.make_async_copy(xt_hbm, xt, sems.at[4])
    loads[0].start()
    load_f.start()
    load_v.start()
    load_b.start()
    for copy in loads[1:]:
        copy.start()
    load_xt.start()
    for b in range(bands):
        r_scr[b * count : (b + 1) * count, :] = r_ref[b].astype(F32)

    for s in range(4):
        loads[s].wait()
        w = jnp.concatenate([r_ref[b] for b in range(bands)], axis=1)
        g = dot(tx[s * 2 * size : (s + 1) * 2 * size, :], w).astype(BF16)
        left = jnp.concatenate(
            [
                jnp.concatenate(
                    [g[:size, b * 128 : (b + 1) * 128], g[size:, b * 128 : (b + 1) * 128]], axis=1
                )
                for b in range(bands)
            ],
            axis=0,
        )
        if s == 0:
            load_f.wait()
            load_v.wait()
            load_b.wait()
        v = jnp.concatenate([v4[s], v4[s]], axis=1)
        field = (dot(left, yf[s]) * jnp.concatenate([v] * bands, axis=0)).astype(BF16)
        back = dot(field, yb[s]).astype(BF16)
        row = s * 2 * size
        for b in range(bands):
            part = back[b * size : (b + 1) * size]
            h[row : row + size, b * 128 : (b + 1) * 128] = part[:, :128]
            h[row + size : row + 2 * size, b * 128 : (b + 1) * 128] = part[:, 128:]

    load_xt.wait()
    sums = {}

    def add(key, value):
        value = value[:8] + value[8:16] + value[16:24]
        sums[key] = sums[key] + value if key in sums else value

    first = 0
    for group in groups:
        for n in reversed(range(bands // 2)):
            out = dot(xt[first * rows : (first + group) * rows, :], h[:, n * 256 : (n + 1) * 256])
            for f in range(group):
                block = out[f * rows : (f + 1) * rows]
                for j in range(2):
                    at = ((2 * n + j) * ffts + first + f) * message
                    p_scr[at : at + rows, :] = block[:, j * 128 : (j + 1) * 128]
                for i in range(2 * n + 2):
                    at = i * count + (first + f) * rows
                    real, imag = r_scr[at : at + blocks, :], r_scr[at + blocks : at + rows, :]
                    for j in range(max(i, 2 * n), 2 * n + 2):
                        part = block[:, (j - 2 * n) * 128 : (j - 2 * n + 1) * 128]
                        add((i, j, 0), real * part[:blocks] + imag * part[blocks:])
                        add((i, j, 1), real * part[blocks:] - imag * part[:blocks])
            if first + group == ffts:
                done = slice(2 * n * ffts * message, (2 * n + 2) * ffts * message)
                o_ref[done, :] = p_scr[done, :].astype(BF16)
        first += group

    sums = {key: jnp.sum(value, axis=0, keepdims=True) for key, value in sums.items()}
    lines = []
    for i in range(bands):
        lines += [sums[min(i, j), max(i, j), 0] for j in range(bands)]
        lines += [sums[i, j, 1] if i <= j else -sums[j, i, 1] for j in range(bands)]
    total = jnp.sum(jnp.transpose(jnp.concatenate(lines, axis=0)), axis=0, keepdims=True)
    high = total.astype(BF16).astype(F32)
    pair = jnp.concatenate([high, total - high], axis=0)
    for b in range(bands):
        part = pair if b == 0 else pltpu.roll(pair, 128 - b * 2 * bands, 1)
        part = part.astype(BF16)
        for f in range(ffts):
            at = (b * ffts + f) * message + rows
            o_ref[at : at + message - rows, :] = part


def call(kernel, out_shape, scratch, flops, args, in_hbm=(), out_hbm=(), limit=40):
    read = sum(a.size * a.dtype.itemsize for a in args)
    outs = out_shape if isinstance(out_shape, tuple) else (out_shape,)
    written = sum(math.prod(s.shape) * jnp.dtype(s.dtype).itemsize for s in outs)
    args = [
        pltpu.with_memory_space_constraint(a, pltpu.HBM) if i in in_hbm else a
        for i, a in enumerate(args)
    ]
    results = pl.pallas_call(
        kernel,
        out_shape=outs,
        in_specs=[HBM if i in in_hbm else VMEM for i in range(len(args))],
        out_specs=[HBM if i in out_hbm else VMEM for i in range(len(outs))],
        scratch_shapes=scratch,
        compiler_params=pltpu.CompilerParams(vmem_limit_bytes=limit * 2**20),
        cost_estimate=pl.CostEstimate(flops=flops, bytes_accessed=read + written, transcendentals=0),
    )(*args)
    return results if isinstance(out_shape, tuple) else results[0]


def body(coeffs, potential, pattern):
    block_count, block_width = coeffs.shape[1], coeffs.shape[2]
    size = coeffs.shape[-1]
    bands, ffts = lax.axis_size("band"), lax.axis_size("fft")
    devices = bands * ffts
    per_dev = size // devices
    sticks = block_count * block_width
    rows = 2 * block_count
    shape = jax.ShapeDtypeStruct

    table = plane_table(size, bands, ffts)
    forward = dft_table(size, 1.0).reshape(2 * size, 2 * size)
    y_forward = split_table(size, 4, per_dev)
    y_backward = np.ascontiguousarray(y_forward.transpose(0, 2, 1))

    sent = call(
        to_planes_kernel,
        pltpu.VMEM((devices * rows, 128), BF16),
        [pltpu.VMEM((devices * rows, 128), F32)],
        2 * sticks * (2 * size) ** 2,
        (coeffs.reshape(sticks, 2 * size), jnp.asarray(np.ascontiguousarray(table.T))),
    )
    got = lax.all_to_all(
        sent.reshape(devices, rows, 128), AXES, split_axis=0, concat_axis=0, tiled=True
    )
    got = got.reshape(bands, ffts * rows, 128)

    order = pattern.reshape(ffts, 1, block_count) * 2 + jnp.arange(2, dtype=jnp.int32)[None, :, None]
    planes = lax.dynamic_slice_in_dim(potential, lax.axis_index("band") * per_dev, per_dev, 0)
    count = ffts * rows
    tables = (
        pltpu.HBM((8 * size, count), BF16),
        pltpu.HBM((count, 8 * size), BF16),
        pltpu.HBM((4, size, per_dev * size // 4), F32),
    )
    held = [pltpu.VMEM(t.shape, t.dtype) for t in tables]
    x_table, x_back, v4 = call(
        prepare_kernel,
        tables,
        held + [pltpu.SemaphoreType.DMA((6,))],
        2 * 2 * 4 * count * (2 * size) ** 2,
        (
            order.reshape(1, count),
            order.reshape(count, 1),
            planes,
            jnp.asarray(forward),
            jnp.asarray(np.ascontiguousarray(forward.T)),
            jnp.asarray(order_table(size, 4, per_dev)),
        ),
        out_hbm=(0, 1, 2),
    )

    message = rows + 2
    picked = call(
        functools.partial(planes_kernel, (16,)),
        shape((devices * message, 128), BF16),
        held
        + [
            pltpu.VMEM(y_forward.shape, BF16),
            pltpu.VMEM(y_forward.shape, BF16),
            pltpu.VMEM((8 * size, bands * 128), BF16),
            pltpu.VMEM((bands * count, 128), F32),
            pltpu.VMEM((devices * message, 128), F32),
            pltpu.SemaphoreType.DMA((8,)),
        ],
        2 * bands * 128 * 2 * 8 * size * count,
        (got, x_table, x_back, v4, jnp.asarray(y_forward), jnp.asarray(y_backward)),
        in_hbm=(1, 2, 3, 4, 5),
    )
    returned = lax.all_to_all(
        picked.reshape(devices, message // 2, 2, 128), AXES, split_axis=0, concat_axis=0, tiled=True
    )

    total_count = block_count * ffts * block_width * size
    images, matrix_rows = call(
        functools.partial(from_planes_kernel, total_count),
        (pltpu.HBM((sticks, 2, size), BF16), shape((2, 1, bands), F32)),
        [
            pltpu.VMEM((devices * message, 128), F32),
            pltpu.VMEM((sticks, 2, size), BF16),
            pltpu.VMEM((2, 512, 128), F32),
            pltpu.VMEM((2, 512, 128), F32),
            pltpu.SemaphoreType.DMA((block_count // 4,)),
        ],
        2 * sticks * (2 * size) ** 2,
        (returned.reshape(devices * message, 128), jnp.asarray(table)),
        out_hbm=(0,),
    )
    return (images.reshape(coeffs.shape), matrix_rows)


def solution(mesh):
    placed = (P("band", "fft", None, None, None), P("fft", None, None), P())
    return jax.shard_map(
        body,
        mesh=mesh,
        in_specs=placed,
        out_specs=(P("band", "fft", None, None, None), P(None, "band", None)),
        check_vma=False,
    )
```

```python
import functools
import math

import jax
import jax.numpy as jnp
import ml_dtypes
import numpy as np
from jax import lax
from jax.experimental import pallas as pl
from jax.experimental.pallas import tpu as pltpu
from jax.sharding import PartitionSpec as P

F32 = jnp.float32
BF16 = jnp.bfloat16
AXES = ("band", "fft")
VMEM = pl.BlockSpec(memory_space=pltpu.VMEM)
HBM = pl.BlockSpec(memory_space=pltpu.HBM)


def dft_table(size, sign):
    counter = np.arange(size)
    angles = (counter[:, None] * counter[None, :] % size) * (2.0 * math.pi / size)
    cosine = np.cos(angles) / math.sqrt(size)
    sine = sign * np.sin(angles) / math.sqrt(size)
    table = np.stack([np.stack([cosine, sine], 1), np.stack([-sine, cosine], 1)], 0)
    return table.astype(ml_dtypes.bfloat16)


def plane_table(size, bands, ffts):
    per_fft = size // ffts
    per_dev = per_fft // bands
    forward = dft_table(size, 1.0)
    p, b, f = np.meshgrid(np.arange(per_dev), np.arange(bands), np.arange(ffts), indexing="ij")
    z = (f * per_fft + b * per_dev + p).reshape(-1)
    rows = forward[:, :, :, z].reshape(2, size, 2, per_dev, bands * ffts)
    return np.ascontiguousarray(rows.transpose(3, 2, 4, 0, 1)).reshape(2 * size, 2 * size)


def split_table(size, parts, per_dev):
    width = size // parts
    forward = dft_table(size, 1.0).astype(np.float32)
    out = np.zeros((parts, 2, per_dev, width, 2, per_dev, width), np.float32)
    for s in range(parts):
        part = forward[:, :width, :, s::parts]
        for p in range(per_dev):
            out[s, :, p, :, :, p, :] = part
    side = 2 * per_dev * width
    return out.reshape(parts, side, side).astype(ml_dtypes.bfloat16)


def order_table(size, parts, per_dev):
    width = size // parts
    out = np.zeros((per_dev, size, parts, per_dev, width), np.float32)
    for p in range(per_dev):
        for y in range(size):
            out[p, y, y % parts, p, y // parts] = 1.0
    return out.reshape(per_dev * size, parts * per_dev * width).astype(ml_dtypes.bfloat16)


def dot(a, b):
    return jnp.dot(a, b, preferred_element_type=F32)


def dot_nt(a, b):
    return lax.dot_general(a, b, (((1,), (1,)), ((), ())), preferred_element_type=F32)


def to_planes_kernel(c_ref, t_ref, o_hbm, out, first, second, sems):
    side = t_ref.shape[1] // 2
    devices = side // 4
    rows = first.shape[0] // devices
    blocks = rows // 2
    copies = []
    for n, scr in enumerate((first, second)):
        for g in range(blocks // 4):
            r = dot(c_ref[g * 256 : (g + 1) * 256, :], t_ref[:, n * side : (n + 1) * side])
            for i in range(4):
                part = r[i * 64 : (i + 1) * 64]
                part = jnp.concatenate([part[:, : side // 2], part[:, side // 2 :]], axis=0)
                part = jnp.transpose(part)
                for d in range(2):
                    at = pl.ds(d * blocks + g * 4 + i, devices, stride=rows)
                    scr[at, :] = part[d * devices : (d + 1) * devices]
        half = pl.ds(n * devices * rows, devices * rows)
        out[half, :] = scr[...].astype(BF16)
        copies.append(pltpu.make_async_copy(out.at[half], o_hbm.at[half], sems.at[n]))
        copies[-1].start()
    for copy in copies:
        copy.wait()


def from_planes_kernel(count, x_ref, t_ref, o_hbm, m_ref, scr, out, pairs0, pairs1, sems):
    devices = t_ref.shape[0] // 4
    rows = scr.shape[0] // devices
    blocks = rows // 2 - 1
    bands = m_ref.shape[2]
    scr[...] = x_ref[...].astype(F32)
    total = sum(scr[pl.ds(2 * blocks + i, devices, stride=rows), :] for i in range(2))
    total = jnp.sum(total, axis=0, keepdims=True) / count
    m_ref[0] = total[:, :bands]
    m_ref[1] = total[:, bands : 2 * bands]
    copies = []
    for g in range(blocks // 4):
        parts = []
        for m in range(g * 4, g * 4 + 4):
            y = jnp.concatenate(
                [scr[pl.ds(d * blocks + m, devices, stride=rows), :] for d in range(2)], axis=0
            )
            y = jnp.transpose(y).astype(BF16)
            parts.append(jnp.concatenate([y[:64], y[64:]], axis=1))
        value = dot(jnp.concatenate(parts, axis=0), t_ref[...])
        pairs = (pairs0, pairs1)[g % 2]
        for d in range(2):
            for k in range(2):
                at = d * 256 + k * 128
                pairs[pl.ds(2 * k + d, 256, stride=4), :] = value[:, at : at + 128]
        part = pl.ds(g * 1024, 1024)
        out[part, :] = pairs[...].astype(BF16)
        copies.append(pltpu.make_async_copy(out.at[part], o_hbm.at[part], sems.at[g]))
        copies[-1].start()
    for copy in copies:
        copy.wait()


def prepare_kernel(
    row_ref, col_ref, v_ref, f_ref, b_ref, ord_ref, tx_hbm, xt_hbm, v4_hbm, tx0, tx, xt, v4, sems
):
    size = f_ref.shape[0] // 2
    count = row_ref.shape[1]

    def hot(code, iota, s, axis):
        turn = (s * ((code >> 1) & 3) + (code & 1)) & 3
        hit = iota == (code >> 3)
        real = jnp.where(turn == 0, 1.0, jnp.where(turn == 2, -1.0, 0.0))
        imag = jnp.where(turn == 1, 1.0, jnp.where(turn == 3, -1.0, 0.0))
        return jnp.concatenate(
            [jnp.where(hit, real, 0.0), jnp.where(hit, imag, 0.0)], axis=axis
        ).astype(BF16)

    copies = []
    rows = lax.broadcasted_iota(jnp.int32, (size, count), 0)
    cols = lax.broadcasted_iota(jnp.int32, (count, size), 1)
    for s in range(4):
        part = slice(s * 2 * size, (s + 1) * 2 * size)
        tx[part, :] = dot(b_ref[...], hot(row_ref[...], rows, s, 0)).astype(BF16)
        if s == 0:
            tx0[...] = tx[part, :]
        else:
            copies.append(pltpu.make_async_copy(tx.at[part], tx_hbm.at[part], sems.at[s]))
            copies[-1].start()
        xt[:, part] = dot(hot(col_ref[...], cols, s, 1), f_ref[...]).astype(BF16)
    copies.append(pltpu.make_async_copy(xt, xt_hbm, sems.at[4]))
    copies[-1].start()
    v = jnp.concatenate([v_ref[0], v_ref[1]], axis=1)
    high = v.astype(BF16)
    rest = (v - high.astype(F32)).astype(BF16)
    both = dot(high, ord_ref[...]) + dot(rest, ord_ref[...])
    for s in range(4):
        v4[s] = both[:, s * 128 : (s + 1) * 128]
    copies.append(pltpu.make_async_copy(v4, v4_hbm, sems.at[5]))
    copies[-1].start()
    for copy in copies:
        copy.wait()


def planes_kernel(
    groups, r_ref, tx0, tx_hbm, xt_hbm, v4_hbm, yf_hbm, yb_hbm, o_ref,
    tx, xt, v4, yf, yb, h, r_scr, p_scr, sems,
):
    size = v4.shape[1]
    bands, count = r_ref.shape[0], r_ref.shape[1]
    ffts = sum(groups)
    rows, blocks = count // ffts, count // ffts // 2
    message = o_ref.shape[0] // (bands * ffts)
    load_v = pltpu.make_async_copy(v4_hbm, v4, sems.at[5])
    load_f = pltpu.make_async_copy(yf_hbm, yf, sems.at[6])
    load_b = pltpu.make_async_copy(yb_hbm, yb, sems.at[7])
    loads = []
    for s in range(1, 4):
        part = slice(s * 2 * size, (s + 1) * 2 * size)
        loads.append(pltpu.make_async_copy(tx_hbm.at[part], tx.at[part], sems.at[s]))
    load_xt = pltpu.make_async_copy(xt_hbm, xt, sems.at[4])
    load_f.start()
    load_v.start()
    load_b.start()
    for copy in loads:
        copy.start()
    load_xt.start()
    for b in range(bands):
        r_scr[b * count : (b + 1) * count, :] = r_ref[b].astype(F32)

    for s in range(4):
        if s > 0:
            loads[s - 1].wait()
        w = jnp.concatenate([r_ref[b] for b in range(bands)], axis=1)
        g = dot(tx0[...] if s == 0 else tx[s * 2 * size : (s + 1) * 2 * size, :], w).astype(BF16)
        left = jnp.concatenate(
            [
                jnp.concatenate(
                    [g[:size, b * 128 : (b + 1) * 128], g[size:, b * 128 : (b + 1) * 128]], axis=1
                )
                for b in range(bands)
            ],
            axis=0,
        )
        if s == 0:
            load_f.wait()
            load_v.wait()
            load_b.wait()
        v = jnp.concatenate([v4[s], v4[s]], axis=1)
        field = (dot(left, yf[s]) * jnp.concatenate([v] * bands, axis=0)).astype(BF16)
        back = dot(field, yb[s]).astype(BF16)
        row = s * 2 * size
        for b in range(bands):
            part = back[b * size : (b + 1) * size]
            h[row : row + size, b * 128 : (b + 1) * 128] = part[:, :128]
            h[row + size : row + 2 * size, b * 128 : (b + 1) * 128] = part[:, 128:]

    load_xt.wait()
    sums = {}

    def add(key, value):
        value = value[:8] + value[8:16] + value[16:24]
        sums[key] = sums[key] + value if key in sums else value

    first = 0
    for group in groups:
        for n in reversed(range(bands // 2)):
            out = dot(xt[first * rows : (first + group) * rows, :], h[:, n * 256 : (n + 1) * 256])
            for f in range(group):
                block = out[f * rows : (f + 1) * rows]
                for j in range(2):
                    at = ((2 * n + j) * ffts + first + f) * message
                    p_scr[at : at + rows, :] = block[:, j * 128 : (j + 1) * 128]
                for i in range(2 * n + 2):
                    at = i * count + (first + f) * rows
                    real, imag = r_scr[at : at + blocks, :], r_scr[at + blocks : at + rows, :]
                    for j in range(max(i, 2 * n), 2 * n + 2):
                        part = block[:, (j - 2 * n) * 128 : (j - 2 * n + 1) * 128]
                        add((i, j, 0), real * part[:blocks] + imag * part[blocks:])
                        add((i, j, 1), real * part[blocks:] - imag * part[:blocks])
            if first + group == ffts:
                done = slice(2 * n * ffts * message, (2 * n + 2) * ffts * message)
                o_ref[done, :] = p_scr[done, :].astype(BF16)
        first += group

    sums = {key: jnp.sum(value, axis=0, keepdims=True) for key, value in sums.items()}
    lines = []
    for i in range(bands):
        lines += [sums[min(i, j), max(i, j), 0] for j in range(bands)]
        lines += [sums[i, j, 1] if i <= j else -sums[j, i, 1] for j in range(bands)]
    total = jnp.sum(jnp.transpose(jnp.concatenate(lines, axis=0)), axis=0, keepdims=True)
    high = total.astype(BF16).astype(F32)
    pair = jnp.concatenate([high, total - high], axis=0)
    for b in range(bands):
        part = pair if b == 0 else pltpu.roll(pair, 128 - b * 2 * bands, 1)
        part = part.astype(BF16)
        for f in range(ffts):
            at = (b * ffts + f) * message + rows
            o_ref[at : at + message - rows, :] = part


def call(kernel, out_shape, scratch, flops, args, in_hbm=(), out_hbm=(), limit=40):
    read = sum(a.size * a.dtype.itemsize for a in args)
    outs = out_shape if isinstance(out_shape, tuple) else (out_shape,)
    written = sum(math.prod(s.shape) * jnp.dtype(s.dtype).itemsize for s in outs)
    args = [
        pltpu.with_memory_space_constraint(a, pltpu.HBM) if i in in_hbm else a
        for i, a in enumerate(args)
    ]
    results = pl.pallas_call(
        kernel,
        out_shape=outs,
        in_specs=[HBM if i in in_hbm else VMEM for i in range(len(args))],
        out_specs=[HBM if i in out_hbm else VMEM for i in range(len(outs))],
        scratch_shapes=scratch,
        compiler_params=pltpu.CompilerParams(vmem_limit_bytes=limit * 2**20),
        cost_estimate=pl.CostEstimate(flops=flops, bytes_accessed=read + written, transcendentals=0),
    )(*args)
    return results if isinstance(out_shape, tuple) else results[0]


def body(coeffs, potential, pattern):
    block_count, block_width = coeffs.shape[1], coeffs.shape[2]
    size = coeffs.shape[-1]
    bands, ffts = lax.axis_size("band"), lax.axis_size("fft")
    devices = bands * ffts
    per_dev = size // devices
    sticks = block_count * block_width
    rows = 2 * block_count
    shape = jax.ShapeDtypeStruct

    table = plane_table(size, bands, ffts)
    halves = table.reshape(2 * per_dev, 2, devices // 2, 2 * size)
    halves = halves.transpose(1, 0, 2, 3).reshape(2 * size, 2 * size)
    forward = dft_table(size, 1.0).reshape(2 * size, 2 * size)
    y_forward = split_table(size, 4, per_dev)
    y_backward = np.ascontiguousarray(y_forward.transpose(0, 2, 1))

    sent = call(
        to_planes_kernel,
        pltpu.HBM((devices * rows, 128), BF16),
        [
            pltpu.VMEM((devices * rows, 128), BF16),
            pltpu.VMEM((devices * rows // 2, 128), F32),
            pltpu.VMEM((devices * rows // 2, 128), F32),
            pltpu.SemaphoreType.DMA((2,)),
        ],
        2 * sticks * (2 * size) ** 2,
        (coeffs.reshape(sticks, 2 * size), jnp.asarray(np.ascontiguousarray(halves.T))),
        out_hbm=(0,),
    )
    got = lax.all_to_all(
        sent.reshape(devices, rows, 128), AXES, split_axis=0, concat_axis=0, tiled=True
    )
    got = got.reshape(bands, ffts * rows, 128)

    order = pattern.reshape(ffts, 1, block_count) * 2 + jnp.arange(2, dtype=jnp.int32)[None, :, None]
    planes = lax.dynamic_slice_in_dim(potential, lax.axis_index("band") * per_dev, per_dev, 0)
    count = ffts * rows
    tables = (
        pltpu.HBM((8 * size, count), BF16),
        pltpu.HBM((count, 8 * size), BF16),
        pltpu.HBM((4, size, per_dev * size // 4), F32),
    )
    held = [pltpu.VMEM(t.shape, t.dtype) for t in tables]
    x_table, x_back, v4, x_first = call(
        prepare_kernel,
        tables + (shape((2 * size, count), BF16),),
        held + [pltpu.SemaphoreType.DMA((6,))],
        2 * 2 * 4 * count * (2 * size) ** 2,
        (
            order.reshape(1, count),
            order.reshape(count, 1),
            planes,
            jnp.asarray(forward),
            jnp.asarray(np.ascontiguousarray(forward.T)),
            jnp.asarray(order_table(size, 4, per_dev)),
        ),
        out_hbm=(0, 1, 2),
    )

    message = rows + 2
    picked = call(
        functools.partial(planes_kernel, (16,)),
        shape((devices * message, 128), BF16),
        held
        + [
            pltpu.VMEM(y_forward.shape, BF16),
            pltpu.VMEM(y_forward.shape, BF16),
            pltpu.VMEM((8 * size, bands * 128), BF16),
            pltpu.VMEM((bands * count, 128), F32),
            pltpu.VMEM((devices * message, 128), F32),
            pltpu.SemaphoreType.DMA((8,)),
        ],
        2 * bands * 128 * 2 * 8 * size * count,
        (got, x_first, x_table, x_back, v4, jnp.asarray(y_forward), jnp.asarray(y_backward)),
        in_hbm=(2, 3, 4, 5, 6),
    )
    returned = lax.all_to_all(
        picked.reshape(devices, message // 2, 2, 128), AXES, split_axis=0, concat_axis=0, tiled=True
    )

    total_count = block_count * ffts * block_width * size
    images, matrix_rows = call(
        functools.partial(from_planes_kernel, total_count),
        (pltpu.HBM((4 * sticks, 128), BF16), shape((2, 1, bands), F32)),
        [
            pltpu.VMEM((devices * message, 128), F32),
            pltpu.VMEM((4 * sticks, 128), BF16),
        ]
        + [pltpu.VMEM((1024, 128), F32)] * 2
        + [pltpu.SemaphoreType.DMA((block_count // 4,))],
        2 * sticks * (2 * size) ** 2,
        (returned.reshape(devices * message, 128), jnp.asarray(table)),
        out_hbm=(0,),
    )
    images = images.reshape(sticks, 2, 2, 128).transpose(0, 2, 1, 3)
    return (images.reshape(coeffs.shape), matrix_rows)


def solution(mesh):
    placed = (P("band", "fft", None, None, None), P("fft", None, None), P())
    return jax.shard_map(
        body,
        mesh=mesh,
        in_specs=placed,
        out_specs=(P("band", "fft", None, None, None), P(None, "band", None)),
        check_vma=False,
    )
```

```python
import functools
import math

import jax
import jax.numpy as jnp
import ml_dtypes
import numpy as np
from jax import lax
from jax.experimental import pallas as pl
from jax.experimental.pallas import tpu as pltpu
from jax.sharding import PartitionSpec as P

F32 = jnp.float32
BF16 = jnp.bfloat16
AXES = ("band", "fft")
VMEM = pl.BlockSpec(memory_space=pltpu.VMEM)
HBM = pl.BlockSpec(memory_space=pltpu.HBM)


def dft_table(size, sign):
    counter = np.arange(size)
    angles = (counter[:, None] * counter[None, :] % size) * (2.0 * math.pi / size)
    cosine = np.cos(angles) / math.sqrt(size)
    sine = sign * np.sin(angles) / math.sqrt(size)
    table = np.stack([np.stack([cosine, sine], 1), np.stack([-sine, cosine], 1)], 0)
    return table.astype(ml_dtypes.bfloat16)


def plane_table(size, bands, ffts):
    per_fft = size // ffts
    per_dev = per_fft // bands
    forward = dft_table(size, 1.0)
    p, b, f = np.meshgrid(np.arange(per_dev), np.arange(bands), np.arange(ffts), indexing="ij")
    z = (f * per_fft + b * per_dev + p).reshape(-1)
    rows = forward[:, :, :, z].reshape(2, size, 2, per_dev, bands * ffts)
    return np.ascontiguousarray(rows.transpose(3, 2, 4, 0, 1)).reshape(2 * size, 2 * size)


def split_table(size, parts, per_dev):
    width = size // parts
    forward = dft_table(size, 1.0).astype(np.float32)
    out = np.zeros((parts, 2, per_dev, width, 2, per_dev, width), np.float32)
    for s in range(parts):
        part = forward[:, :width, :, s::parts]
        for p in range(per_dev):
            out[s, :, p, :, :, p, :] = part
    side = 2 * per_dev * width
    return out.reshape(parts, side, side).astype(ml_dtypes.bfloat16)


def order_table(size, parts, per_dev):
    width = size // parts
    out = np.zeros((per_dev, size, parts, per_dev, width), np.float32)
    for p in range(per_dev):
        for y in range(size):
            out[p, y, y % parts, p, y // parts] = 1.0
    return out.reshape(per_dev * size, parts * per_dev * width).astype(ml_dtypes.bfloat16)


def dot(a, b):
    return jnp.dot(a, b, preferred_element_type=F32)


def dot_nt(a, b):
    return lax.dot_general(a, b, (((1,), (1,)), ((), ())), preferred_element_type=F32)


def to_planes_kernel(c_ref, t_ref, o_hbm, out, first, second, sems):
    side = t_ref.shape[1] // 2
    devices = side // 4
    rows = first.shape[0] // devices
    blocks = rows // 2
    copies = []
    for n, scr in enumerate((first, second)):
        for g in range(blocks // 4):
            r = dot(c_ref[g * 256 : (g + 1) * 256, :], t_ref[:, n * side : (n + 1) * side])
            for i in range(4):
                part = r[i * 64 : (i + 1) * 64]
                part = jnp.concatenate([part[:, : side // 2], part[:, side // 2 :]], axis=0)
                part = jnp.transpose(part)
                for d in range(2):
                    at = pl.ds(d * blocks + g * 4 + i, devices, stride=rows)
                    scr[at, :] = part[d * devices : (d + 1) * devices]
        half = pl.ds(n * devices * rows, devices * rows)
        out[half, :] = scr[...].astype(BF16)
        copies.append(pltpu.make_async_copy(out.at[half], o_hbm.at[half], sems.at[n]))
        copies[-1].start()
    for copy in copies:
        copy.wait()


def from_planes_kernel(count, x_ref, t_ref, o_hbm, m_ref, scr, out, pairs0, pairs1, sems):
    devices = t_ref.shape[0] // 4
    rows = scr.shape[0] // devices
    blocks = rows // 2 - 1
    bands = m_ref.shape[2]
    scr[...] = x_ref[...].astype(F32)
    total = sum(scr[pl.ds(2 * blocks + i, devices, stride=rows), :] for i in range(2))
    total = jnp.sum(total, axis=0, keepdims=True) / count
    m_ref[0] = total[:, :bands]
    m_ref[1] = total[:, bands : 2 * bands]
    copies = []
    for g in range(blocks // 4):
        parts = []
        for m in range(g * 4, g * 4 + 4):
            y = jnp.concatenate(
                [scr[pl.ds(d * blocks + m, devices, stride=rows), :] for d in range(2)], axis=0
            )
            y = jnp.transpose(y).astype(BF16)
            parts.append(jnp.concatenate([y[:64], y[64:]], axis=1))
        value = dot(jnp.concatenate(parts, axis=0), t_ref[...])
        pairs = (pairs0, pairs1)[g % 2]
        for d in range(2):
            for k in range(2):
                at = d * 256 + k * 128
                pairs[pl.ds(2 * k + d, 256, stride=4), :] = value[:, at : at + 128]
        part = pl.ds(g * 1024, 1024)
        out[part, :] = pairs[...].astype(BF16)
        copies.append(pltpu.make_async_copy(out.at[part], o_hbm.at[part], sems.at[g]))
        copies[-1].start()
    for copy in copies:
        copy.wait()


def prepare_kernel(
    row_ref, col_ref, v_ref, f_ref, b_ref, ord_ref, tx_hbm, xt_hbm, v4_hbm, tx, xt, v4, sems
):
    size = f_ref.shape[0] // 2
    count = row_ref.shape[1]

    def hot(code, iota, s, axis):
        turn = (s * ((code >> 1) & 3) + (code & 1)) & 3
        hit = iota == (code >> 3)
        real = jnp.where(turn == 0, 1.0, jnp.where(turn == 2, -1.0, 0.0))
        imag = jnp.where(turn == 1, 1.0, jnp.where(turn == 3, -1.0, 0.0))
        return jnp.concatenate(
            [jnp.where(hit, real, 0.0), jnp.where(hit, imag, 0.0)], axis=axis
        ).astype(BF16)

    copies = []
    rows = lax.broadcasted_iota(jnp.int32, (size, count), 0)
    cols = lax.broadcasted_iota(jnp.int32, (count, size), 1)
    for s in range(4):
        part = slice(s * 2 * size, (s + 1) * 2 * size)
        tx[part, :] = dot(b_ref[...], hot(row_ref[...], rows, s, 0)).astype(BF16)
        copies.append(pltpu.make_async_copy(tx.at[part], tx_hbm.at[part], sems.at[s]))
        copies[-1].start()
        xt[:, part] = dot(hot(col_ref[...], cols, s, 1), f_ref[...]).astype(BF16)
    copies.append(pltpu.make_async_copy(xt, xt_hbm, sems.at[4]))
    copies[-1].start()
    v = jnp.concatenate([v_ref[0], v_ref[1]], axis=1)
    high = v.astype(BF16)
    rest = (v - high.astype(F32)).astype(BF16)
    both = dot(high, ord_ref[...]) + dot(rest, ord_ref[...])
    for s in range(4):
        v4[s] = both[:, s * 128 : (s + 1) * 128]
    copies.append(pltpu.make_async_copy(v4, v4_hbm, sems.at[5]))
    copies[-1].start()
    for copy in copies:
        copy.wait()


def planes_kernel(
    groups, r_ref, tx_hbm, xt_hbm, v4_hbm, yf_hbm, yb_hbm, o_ref,
    tx, xt, v4, yf, yb, h, r_scr, p_scr, sems,
):
    size = v4.shape[1]
    bands, count = r_ref.shape[0], r_ref.shape[1]
    ffts = sum(groups)
    rows, blocks = count // ffts, count // ffts // 2
    message = o_ref.shape[0] // (bands * ffts)
    load_v = pltpu.make_async_copy(v4_hbm, v4, sems.at[5])
    load_f = pltpu.make_async_copy(yf_hbm, yf, sems.at[6])
    load_b = pltpu.make_async_copy(yb_hbm, yb, sems.at[7])
    loads = []
    for s in range(4):
        part = slice(s * 2 * size, (s + 1) * 2 * size)
        loads.append(pltpu.make_async_copy(tx_hbm.at[part], tx.at[part], sems.at[s]))
    load_xt = pltpu.make_async_copy(xt_hbm, xt, sems.at[4])
    loads[0].start()
    load_f.start()
    load_v.start()
    load_b.start()
    for copy in loads[1:]:
        copy.start()
    load_xt.start()
    for b in range(bands):
        r_scr[b * count : (b + 1) * count, :] = r_ref[b].astype(F32)

    for s in range(4):
        loads[s].wait()
        w = jnp.concatenate([r_ref[b] for b in range(bands)], axis=1)
        g = dot(tx[s * 2 * size : (s + 1) * 2 * size, :], w).astype(BF16)
        left = jnp.concatenate(
            [
                jnp.concatenate(
                    [g[:size, b * 128 : (b + 1) * 128], g[size:, b * 128 : (b + 1) * 128]], axis=1
                )
                for b in range(bands)
            ],
            axis=0,
        )
        if s == 0:
            load_f.wait()
            load_v.wait()
            load_b.wait()
        v = jnp.concatenate([v4[s], v4[s]], axis=1)
        field = (dot(left, yf[s]) * jnp.concatenate([v] * bands, axis=0)).astype(BF16)
        back = dot(field, yb[s]).astype(BF16)
        row = s * 2 * size
        for b in range(bands):
            part = back[b * size : (b + 1) * size]
            h[row : row + size, b * 128 : (b + 1) * 128] = part[:, :128]
            h[row + size : row + 2 * size, b * 128 : (b + 1) * 128] = part[:, 128:]

    load_xt.wait()
    sums = {}

    def add(key, value):
        value = value[:8] + value[8:16] + value[16:24]
        sums[key] = sums[key] + value if key in sums else value

    first = 0
    for group in groups:
        for n in reversed(range(bands // 2)):
            out = dot(xt[first * rows : (first + group) * rows, :], h[:, n * 256 : (n + 1) * 256])
            for f in range(group):
                block = out[f * rows : (f + 1) * rows]
                for j in range(2):
                    at = ((2 * n + j) * ffts + first + f) * message
                    p_scr[at : at + rows, :] = block[:, j * 128 : (j + 1) * 128]
                for i in range(2 * n + 2):
                    at = i * count + (first + f) * rows
                    real, imag = r_scr[at : at + blocks, :], r_scr[at + blocks : at + rows, :]
                    for j in range(max(i, 2 * n), 2 * n + 2):
                        part = block[:, (j - 2 * n) * 128 : (j - 2 * n + 1) * 128]
                        add((i, j, 0), real * part[:blocks] + imag * part[blocks:])
                        add((i, j, 1), real * part[blocks:] - imag * part[:blocks])
            if first + group == ffts:
                done = slice(2 * n * ffts * message, (2 * n + 2) * ffts * message)
                o_ref[done, :] = p_scr[done, :].astype(BF16)
        first += group

    sums = {key: jnp.sum(value, axis=0, keepdims=True) for key, value in sums.items()}
    lines = []
    for i in range(bands):
        lines += [sums[min(i, j), max(i, j), 0] for j in range(bands)]
        lines += [sums[i, j, 1] if i <= j else -sums[j, i, 1] for j in range(bands)]
    total = jnp.sum(jnp.transpose(jnp.concatenate(lines, axis=0)), axis=0, keepdims=True)
    high = total.astype(BF16).astype(F32)
    pair = jnp.concatenate([high, total - high], axis=0)
    for b in range(bands):
        part = pair if b == 0 else pltpu.roll(pair, 128 - b * 2 * bands, 1)
        part = part.astype(BF16)
        for f in range(ffts):
            at = (b * ffts + f) * message + rows
            o_ref[at : at + message - rows, :] = part


def call(kernel, out_shape, scratch, flops, args, in_hbm=(), out_hbm=(), limit=40):
    read = sum(a.size * a.dtype.itemsize for a in args)
    outs = out_shape if isinstance(out_shape, tuple) else (out_shape,)
    written = sum(math.prod(s.shape) * jnp.dtype(s.dtype).itemsize for s in outs)
    args = [
        pltpu.with_memory_space_constraint(a, pltpu.HBM) if i in in_hbm else a
        for i, a in enumerate(args)
    ]
    results = pl.pallas_call(
        kernel,
        out_shape=outs,
        in_specs=[HBM if i in in_hbm else VMEM for i in range(len(args))],
        out_specs=[HBM if i in out_hbm else VMEM for i in range(len(outs))],
        scratch_shapes=scratch,
        compiler_params=pltpu.CompilerParams(vmem_limit_bytes=limit * 2**20),
        cost_estimate=pl.CostEstimate(flops=flops, bytes_accessed=read + written, transcendentals=0),
    )(*args)
    return results if isinstance(out_shape, tuple) else results[0]


def body(coeffs, potential, pattern):
    block_count, block_width = coeffs.shape[1], coeffs.shape[2]
    size = coeffs.shape[-1]
    bands, ffts = lax.axis_size("band"), lax.axis_size("fft")
    devices = bands * ffts
    per_dev = size // devices
    sticks = block_count * block_width
    rows = 2 * block_count
    shape = jax.ShapeDtypeStruct

    table = plane_table(size, bands, ffts)
    halves = table.reshape(2 * per_dev, 2, devices // 2, 2 * size)
    halves = halves.transpose(1, 0, 2, 3).reshape(2 * size, 2 * size)
    forward = dft_table(size, 1.0).reshape(2 * size, 2 * size)
    y_forward = split_table(size, 4, per_dev)
    y_backward = np.ascontiguousarray(y_forward.transpose(0, 2, 1))

    sent = call(
        to_planes_kernel,
        pltpu.HBM((devices * rows, 128), BF16),
        [
            pltpu.VMEM((devices * rows, 128), BF16),
            pltpu.VMEM((devices * rows // 2, 128), F32),
            pltpu.VMEM((devices * rows // 2, 128), F32),
            pltpu.SemaphoreType.DMA((2,)),
        ],
        2 * sticks * (2 * size) ** 2,
        (coeffs.reshape(sticks, 2 * size), jnp.asarray(np.ascontiguousarray(halves.T))),
        out_hbm=(0,),
    )
    got = lax.all_to_all(
        sent.reshape(devices, rows, 128), AXES, split_axis=0, concat_axis=0, tiled=True
    )
    got = got.reshape(bands, ffts * rows, 128)

    order = pattern.reshape(ffts, 1, block_count) * 2 + jnp.arange(2, dtype=jnp.int32)[None, :, None]
    planes = lax.dynamic_slice_in_dim(potential, lax.axis_index("band") * per_dev, per_dev, 0)
    count = ffts * rows
    tables = (
        pltpu.HBM((8 * size, count), BF16),
        pltpu.HBM((count, 8 * size), BF16),
        pltpu.HBM((4, size, per_dev * size // 4), F32),
    )
    held = [pltpu.VMEM(t.shape, t.dtype) for t in tables]
    x_table, x_back, v4 = call(
        prepare_kernel,
        tables,
        held + [pltpu.SemaphoreType.DMA((6,))],
        2 * 2 * 4 * count * (2 * size) ** 2,
        (
            order.reshape(1, count),
            order.reshape(count, 1),
            planes,
            jnp.asarray(forward),
            jnp.asarray(np.ascontiguousarray(forward.T)),
            jnp.asarray(order_table(size, 4, per_dev)),
        ),
        out_hbm=(0, 1, 2),
    )

    message = rows + 2
    picked = call(
        functools.partial(planes_kernel, (16,)),
        shape((devices * message, 128), BF16),
        held
        + [
            pltpu.VMEM(y_forward.shape, BF16),
            pltpu.VMEM(y_forward.shape, BF16),
            pltpu.VMEM((8 * size, bands * 128), BF16),
            pltpu.VMEM((bands * count, 128), F32),
            pltpu.VMEM((devices * message, 128), F32),
            pltpu.SemaphoreType.DMA((8,)),
        ],
        2 * bands * 128 * 2 * 8 * size * count,
        (got, x_table, x_back, v4, jnp.asarray(y_forward), jnp.asarray(y_backward)),
        in_hbm=(1, 2, 3, 4, 5),
    )
    returned = lax.all_to_all(
        picked.reshape(devices, message // 2, 2, 128), AXES, split_axis=0, concat_axis=0, tiled=True
    )

    total_count = block_count * ffts * block_width * size
    images, matrix_rows = call(
        functools.partial(from_planes_kernel, total_count),
        (pltpu.HBM((4 * sticks, 128), BF16), shape((2, 1, bands), F32)),
        [
            pltpu.VMEM((devices * message, 128), F32),
            pltpu.VMEM((4 * sticks, 128), BF16),
        ]
        + [pltpu.VMEM((1024, 128), F32)] * 2
        + [pltpu.SemaphoreType.DMA((block_count // 4,))],
        2 * sticks * (2 * size) ** 2,
        (returned.reshape(devices * message, 128), jnp.asarray(table)),
        out_hbm=(0,),
    )
    images = images.reshape(sticks, 2, 2, 128).transpose(0, 2, 1, 3)
    return (images.reshape(coeffs.shape), matrix_rows)


def solution(mesh):
    placed = (P("band", "fft", None, None, None), P("fft", None, None), P())
    return jax.shard_map(
        body,
        mesh=mesh,
        in_specs=placed,
        out_specs=(P("band", "fft", None, None, None), P(None, "band", None)),
        check_vma=False,
    )
```

```python
import functools
import math

import jax
import jax.numpy as jnp
import ml_dtypes
import numpy as np
from jax import lax
from jax.experimental import pallas as pl
from jax.experimental.pallas import tpu as pltpu
from jax.sharding import PartitionSpec as P

F32 = jnp.float32
BF16 = jnp.bfloat16
AXES = ("band", "fft")
VMEM = pl.BlockSpec(memory_space=pltpu.VMEM)
HBM = pl.BlockSpec(memory_space=pltpu.HBM)


def dft_table(size, sign):
    counter = np.arange(size)
    angles = (counter[:, None] * counter[None, :] % size) * (2.0 * math.pi / size)
    cosine = np.cos(angles) / math.sqrt(size)
    sine = sign * np.sin(angles) / math.sqrt(size)
    table = np.stack([np.stack([cosine, sine], 1), np.stack([-sine, cosine], 1)], 0)
    return table.astype(ml_dtypes.bfloat16)


def plane_table(size, bands, ffts):
    per_fft = size // ffts
    per_dev = per_fft // bands
    forward = dft_table(size, 1.0)
    p, b, f = np.meshgrid(np.arange(per_dev), np.arange(bands), np.arange(ffts), indexing="ij")
    z = (f * per_fft + b * per_dev + p).reshape(-1)
    rows = forward[:, :, :, z].reshape(2, size, 2, per_dev, bands * ffts)
    return np.ascontiguousarray(rows.transpose(3, 2, 4, 0, 1)).reshape(2 * size, 2 * size)


def split_table(size, parts, per_dev):
    width = size // parts
    forward = dft_table(size, 1.0).astype(np.float32)
    out = np.zeros((parts, 2, per_dev, width, 2, per_dev, width), np.float32)
    for s in range(parts):
        part = forward[:, :width, :, s::parts]
        for p in range(per_dev):
            out[s, :, p, :, :, p, :] = part
    side = 2 * per_dev * width
    return out.reshape(parts, side, side).astype(ml_dtypes.bfloat16)


def order_table(size, parts, per_dev):
    width = size // parts
    out = np.zeros((per_dev, size, parts, per_dev, width), np.float32)
    for p in range(per_dev):
        for y in range(size):
            out[p, y, y % parts, p, y // parts] = 1.0
    return out.reshape(per_dev * size, parts * per_dev * width).astype(ml_dtypes.bfloat16)


def dot(a, b):
    return jnp.dot(a, b, preferred_element_type=F32)


def dot_nt(a, b):
    return lax.dot_general(a, b, (((1,), (1,)), ((), ())), preferred_element_type=F32)


def to_planes_kernel(c_ref, t_ref, o_hbm, out, first, second, sems):
    side = t_ref.shape[1] // 2
    devices = side // 4
    rows = first.shape[0] // devices
    blocks = rows // 2
    copies = []
    for n, scr in enumerate((first, second)):
        for g in range(blocks // 4):
            r = dot(c_ref[g * 256 : (g + 1) * 256, :], t_ref[:, n * side : (n + 1) * side])
            for i in range(4):
                part = r[i * 64 : (i + 1) * 64]
                part = jnp.concatenate([part[:, : side // 2], part[:, side // 2 :]], axis=0)
                part = jnp.transpose(part)
                for d in range(2):
                    at = pl.ds(d * blocks + g * 4 + i, devices, stride=rows)
                    scr[at, :] = part[d * devices : (d + 1) * devices]
        half = pl.ds(n * devices * rows, devices * rows)
        out[half, :] = scr[...].astype(BF16)
        copies.append(pltpu.make_async_copy(out.at[half], o_hbm.at[half], sems.at[n]))
        copies[-1].start()
    for copy in copies:
        copy.wait()


def from_planes_kernel(count, x_ref, t_ref, o_hbm, m_ref, scr, out, pairs0, pairs1, sems):
    devices = t_ref.shape[0] // 4
    rows = scr.shape[0] // devices
    blocks = rows // 2 - 1
    bands = m_ref.shape[2]
    scr[...] = x_ref[...].astype(F32)
    total = sum(scr[pl.ds(2 * blocks + i, devices, stride=rows), :] for i in range(2))
    total = jnp.sum(total, axis=0, keepdims=True) / count
    m_ref[0] = total[:, :bands]
    m_ref[1] = total[:, bands : 2 * bands]
    copies = []
    for g in range(blocks // 4):
        parts = []
        for m in range(g * 4, g * 4 + 4):
            y = jnp.concatenate(
                [scr[pl.ds(d * blocks + m, devices, stride=rows), :] for d in range(2)], axis=0
            )
            y = jnp.transpose(y).astype(BF16)
            parts.append(jnp.concatenate([y[:64], y[64:]], axis=1))
        value = dot(jnp.concatenate(parts, axis=0), t_ref[...])
        pairs = (pairs0, pairs1)[g % 2]
        for d in range(2):
            for k in range(2):
                at = d * 256 + k * 128
                pairs[pl.ds(2 * k + d, 256, stride=4), :] = value[:, at : at + 128]
        part = pl.ds(g * 1024, 1024)
        out[part, :] = pairs[...].astype(BF16)
        copies.append(pltpu.make_async_copy(out.at[part], o_hbm.at[part], sems.at[g]))
        copies[-1].start()
    for copy in copies:
        copy.wait()


def prepare_kernel(
    row_ref, col_ref, v_ref, f_ref, b_ref, ord_ref, tx_hbm, xt_hbm, v4_hbm, tx, xt, v4, sems
):
    size = f_ref.shape[0] // 2
    count = row_ref.shape[1]

    def hot(code, iota, s, axis):
        turn = (s * ((code >> 1) & 3) + (code & 1)) & 3
        hit = iota == (code >> 3)
        real = jnp.where(turn == 0, 1.0, jnp.where(turn == 2, -1.0, 0.0))
        imag = jnp.where(turn == 1, 1.0, jnp.where(turn == 3, -1.0, 0.0))
        return jnp.concatenate(
            [jnp.where(hit, real, 0.0), jnp.where(hit, imag, 0.0)], axis=axis
        ).astype(BF16)

    copies = []
    rows = lax.broadcasted_iota(jnp.int32, (size, count), 0)
    cols = lax.broadcasted_iota(jnp.int32, (count, size), 1)
    for s in range(4):
        part = slice(s * 2 * size, (s + 1) * 2 * size)
        tx[part, :] = dot(b_ref[...], hot(row_ref[...], rows, s, 0)).astype(BF16)
        copies.append(pltpu.make_async_copy(tx.at[part], tx_hbm.at[part], sems.at[s]))
        copies[-1].start()
        xt[:, part] = dot(hot(col_ref[...], cols, s, 1), f_ref[...]).astype(BF16)
    copies.append(pltpu.make_async_copy(xt, xt_hbm, sems.at[4]))
    copies[-1].start()
    v = jnp.concatenate([v_ref[0], v_ref[1]], axis=1)
    high = v.astype(BF16)
    rest = (v - high.astype(F32)).astype(BF16)
    both = dot(high, ord_ref[...]) + dot(rest, ord_ref[...])
    for s in range(4):
        v4[s] = both[:, s * 128 : (s + 1) * 128]
    copies.append(pltpu.make_async_copy(v4, v4_hbm, sems.at[5]))
    copies[-1].start()
    for copy in copies:
        copy.wait()


def planes_kernel(
    groups, r_ref, tx_hbm, xt_hbm, v4_hbm, yf_hbm, yb_hbm, o_ref,
    tx, xt, v4, yf, yb, h, r_scr, p_scr, sems,
):
    size = v4.shape[1]
    bands, count = r_ref.shape[0], r_ref.shape[1]
    ffts = sum(groups)
    rows, blocks = count // ffts, count // ffts // 2
    message = o_ref.shape[0] // (bands * ffts)
    load_v = pltpu.make_async_copy(v4_hbm, v4, sems.at[5])
    load_f = pltpu.make_async_copy(yf_hbm, yf, sems.at[6])
    load_b = pltpu.make_async_copy(yb_hbm, yb, sems.at[7])
    loads = []
    quarters = []
    for i in range(4):
        part = slice(i * size // 2, (i + 1) * size // 2)
        quarters.append(pltpu.make_async_copy(tx_hbm.at[part], tx.at[part], sems.at[8 + i]))
    for s in range(1, 4):
        part = slice(s * 2 * size, (s + 1) * 2 * size)
        loads.append(pltpu.make_async_copy(tx_hbm.at[part], tx.at[part], sems.at[s]))
    load_xt = pltpu.make_async_copy(xt_hbm, xt, sems.at[4])
    for copy in quarters:
        copy.start()
    load_f.start()
    load_v.start()
    load_b.start()
    for copy in loads:
        copy.start()
    load_xt.start()
    for b in range(bands):
        r_scr[b * count : (b + 1) * count, :] = r_ref[b].astype(F32)

    for s in range(4):
        for copy in (quarters, [], loads[1:], [])[s]:
            copy.wait()
        w = jnp.concatenate([r_ref[b] for b in range(bands)], axis=1)
        g = dot(tx[s * 2 * size : (s + 1) * 2 * size, :], w).astype(BF16)
        left = jnp.concatenate(
            [
                jnp.concatenate(
                    [g[:size, b * 128 : (b + 1) * 128], g[size:, b * 128 : (b + 1) * 128]], axis=1
                )
                for b in range(bands)
            ],
            axis=0,
        )
        if s == 0:
            load_f.wait()
            load_v.wait()
            load_b.wait()
            loads[0].wait()
        v = jnp.concatenate([v4[s], v4[s]], axis=1)
        field = (dot(left, yf[s]) * jnp.concatenate([v] * bands, axis=0)).astype(BF16)
        back = dot(field, yb[s]).astype(BF16)
        row = s * 2 * size
        for b in range(bands):
            part = back[b * size : (b + 1) * size]
            h[row : row + size, b * 128 : (b + 1) * 128] = part[:, :128]
            h[row + size : row + 2 * size, b * 128 : (b + 1) * 128] = part[:, 128:]

    load_xt.wait()
    sums = {}

    def add(key, value):
        value = value[:8] + value[8:16] + value[16:24]
        sums[key] = sums[key] + value if key in sums else value

    first = 0
    for group in groups:
        for n in reversed(range(bands // 2)):
            out = dot(xt[first * rows : (first + group) * rows, :], h[:, n * 256 : (n + 1) * 256])
            for f in range(group):
                block = out[f * rows : (f + 1) * rows]
                for j in range(2):
                    at = ((2 * n + j) * ffts + first + f) * message
                    p_scr[at : at + rows, :] = block[:, j * 128 : (j + 1) * 128]
                for i in range(2 * n + 2):
                    at = i * count + (first + f) * rows
                    real, imag = r_scr[at : at + blocks, :], r_scr[at + blocks : at + rows, :]
                    for j in range(max(i, 2 * n), 2 * n + 2):
                        part = block[:, (j - 2 * n) * 128 : (j - 2 * n + 1) * 128]
                        add((i, j, 0), real * part[:blocks] + imag * part[blocks:])
                        add((i, j, 1), real * part[blocks:] - imag * part[:blocks])
            if first + group == ffts:
                done = slice(2 * n * ffts * message, (2 * n + 2) * ffts * message)
                o_ref[done, :] = p_scr[done, :].astype(BF16)
        first += group

    sums = {key: jnp.sum(value, axis=0, keepdims=True) for key, value in sums.items()}
    lines = []
    for i in range(bands):
        lines += [sums[min(i, j), max(i, j), 0] for j in range(bands)]
        lines += [sums[i, j, 1] if i <= j else -sums[j, i, 1] for j in range(bands)]
    total = jnp.sum(jnp.transpose(jnp.concatenate(lines, axis=0)), axis=0, keepdims=True)
    high = total.astype(BF16).astype(F32)
    pair = jnp.concatenate([high, total - high], axis=0)
    for b in range(bands):
        part = pair if b == 0 else pltpu.roll(pair, 128 - b * 2 * bands, 1)
        part = part.astype(BF16)
        for f in range(ffts):
            at = (b * ffts + f) * message + rows
            o_ref[at : at + message - rows, :] = part


def call(kernel, out_shape, scratch, flops, args, in_hbm=(), out_hbm=(), limit=40):
    read = sum(a.size * a.dtype.itemsize for a in args)
    outs = out_shape if isinstance(out_shape, tuple) else (out_shape,)
    written = sum(math.prod(s.shape) * jnp.dtype(s.dtype).itemsize for s in outs)
    args = [
        pltpu.with_memory_space_constraint(a, pltpu.HBM) if i in in_hbm else a
        for i, a in enumerate(args)
    ]
    results = pl.pallas_call(
        kernel,
        out_shape=outs,
        in_specs=[HBM if i in in_hbm else VMEM for i in range(len(args))],
        out_specs=[HBM if i in out_hbm else VMEM for i in range(len(outs))],
        scratch_shapes=scratch,
        compiler_params=pltpu.CompilerParams(vmem_limit_bytes=limit * 2**20),
        cost_estimate=pl.CostEstimate(flops=flops, bytes_accessed=read + written, transcendentals=0),
    )(*args)
    return results if isinstance(out_shape, tuple) else results[0]


def body(coeffs, potential, pattern):
    block_count, block_width = coeffs.shape[1], coeffs.shape[2]
    size = coeffs.shape[-1]
    bands, ffts = lax.axis_size("band"), lax.axis_size("fft")
    devices = bands * ffts
    per_dev = size // devices
    sticks = block_count * block_width
    rows = 2 * block_count
    shape = jax.ShapeDtypeStruct

    table = plane_table(size, bands, ffts)
    halves = table.reshape(2 * per_dev, 2, devices // 2, 2 * size)
    halves = halves.transpose(1, 0, 2, 3).reshape(2 * size, 2 * size)
    forward = dft_table(size, 1.0).reshape(2 * size, 2 * size)
    y_forward = split_table(size, 4, per_dev)
    y_backward = np.ascontiguousarray(y_forward.transpose(0, 2, 1))

    sent = call(
        to_planes_kernel,
        pltpu.HBM((devices * rows, 128), BF16),
        [
            pltpu.VMEM((devices * rows, 128), BF16),
            pltpu.VMEM((devices * rows // 2, 128), F32),
            pltpu.VMEM((devices * rows // 2, 128), F32),
            pltpu.SemaphoreType.DMA((2,)),
        ],
        2 * sticks * (2 * size) ** 2,
        (coeffs.reshape(sticks, 2 * size), jnp.asarray(np.ascontiguousarray(halves.T))),
        out_hbm=(0,),
    )
    got = lax.all_to_all(
        sent.reshape(devices, rows, 128), AXES, split_axis=0, concat_axis=0, tiled=True
    )
    got = got.reshape(bands, ffts * rows, 128)

    order = pattern.reshape(ffts, 1, block_count) * 2 + jnp.arange(2, dtype=jnp.int32)[None, :, None]
    planes = lax.dynamic_slice_in_dim(potential, lax.axis_index("band") * per_dev, per_dev, 0)
    count = ffts * rows
    tables = (
        pltpu.HBM((8 * size, count), BF16),
        pltpu.HBM((count, 8 * size), BF16),
        pltpu.HBM((4, size, per_dev * size // 4), F32),
    )
    held = [pltpu.VMEM(t.shape, t.dtype) for t in tables]
    x_table, x_back, v4 = call(
        prepare_kernel,
        tables,
        held + [pltpu.SemaphoreType.DMA((6,))],
        2 * 2 * 4 * count * (2 * size) ** 2,
        (
            order.reshape(1, count),
            order.reshape(count, 1),
            planes,
            jnp.asarray(forward),
            jnp.asarray(np.ascontiguousarray(forward.T)),
            jnp.asarray(order_table(size, 4, per_dev)),
        ),
        out_hbm=(0, 1, 2),
    )

    message = rows + 2
    picked = call(
        functools.partial(planes_kernel, (16,)),
        shape((devices * message, 128), BF16),
        held
        + [
            pltpu.VMEM(y_forward.shape, BF16),
            pltpu.VMEM(y_forward.shape, BF16),
            pltpu.VMEM((8 * size, bands * 128), BF16),
            pltpu.VMEM((bands * count, 128), F32),
            pltpu.VMEM((devices * message, 128), F32),
            pltpu.SemaphoreType.DMA((12,)),
        ],
        2 * bands * 128 * 2 * 8 * size * count,
        (got, x_table, x_back, v4, jnp.asarray(y_forward), jnp.asarray(y_backward)),
        in_hbm=(1, 2, 3, 4, 5),
    )
    returned = lax.all_to_all(
        picked.reshape(devices, message // 2, 2, 128), AXES, split_axis=0, concat_axis=0, tiled=True
    )

    total_count = block_count * ffts * block_width * size
    images, matrix_rows = call(
        functools.partial(from_planes_kernel, total_count),
        (pltpu.HBM((4 * sticks, 128), BF16), shape((2, 1, bands), F32)),
        [
            pltpu.VMEM((devices * message, 128), F32),
            pltpu.VMEM((4 * sticks, 128), BF16),
        ]
        + [pltpu.VMEM((1024, 128), F32)] * 2
        + [pltpu.SemaphoreType.DMA((block_count // 4,))],
        2 * sticks * (2 * size) ** 2,
        (returned.reshape(devices * message, 128), jnp.asarray(table)),
        out_hbm=(0,),
    )
    images = images.reshape(sticks, 2, 2, 128).transpose(0, 2, 1, 3)
    return (images.reshape(coeffs.shape), matrix_rows)


def solution(mesh):
    placed = (P("band", "fft", None, None, None), P("fft", None, None), P())
    return jax.shard_map(
        body,
        mesh=mesh,
        in_specs=placed,
        out_specs=(P("band", "fft", None, None, None), P(None, "band", None)),
        check_vma=False,
    )
```

```python
import functools
import math

import jax
import jax.numpy as jnp
import ml_dtypes
import numpy as np
from jax import lax
from jax.experimental import pallas as pl
from jax.experimental.pallas import tpu as pltpu
from jax.sharding import PartitionSpec as P

F32 = jnp.float32
BF16 = jnp.bfloat16
AXES = ("band", "fft")
VMEM = pl.BlockSpec(memory_space=pltpu.VMEM)
HBM = pl.BlockSpec(memory_space=pltpu.HBM)


def dft_table(size, sign):
    counter = np.arange(size)
    angles = (counter[:, None] * counter[None, :] % size) * (2.0 * math.pi / size)
    cosine = np.cos(angles) / math.sqrt(size)
    sine = sign * np.sin(angles) / math.sqrt(size)
    table = np.stack([np.stack([cosine, sine], 1), np.stack([-sine, cosine], 1)], 0)
    return table.astype(ml_dtypes.bfloat16)


def plane_table(size, bands, ffts):
    per_fft = size // ffts
    per_dev = per_fft // bands
    forward = dft_table(size, 1.0)
    p, b, f = np.meshgrid(np.arange(per_dev), np.arange(bands), np.arange(ffts), indexing="ij")
    z = (f * per_fft + b * per_dev + p).reshape(-1)
    rows = forward[:, :, :, z].reshape(2, size, 2, per_dev, bands * ffts)
    return np.ascontiguousarray(rows.transpose(3, 2, 4, 0, 1)).reshape(2 * size, 2 * size)


def split_table(size, parts, per_dev):
    width = size // parts
    forward = dft_table(size, 1.0).astype(np.float32)
    out = np.zeros((parts, 2, per_dev, width, 2, per_dev, width), np.float32)
    for s in range(parts):
        part = forward[:, :width, :, s::parts]
        for p in range(per_dev):
            out[s, :, p, :, :, p, :] = part
    side = 2 * per_dev * width
    return out.reshape(parts, side, side).astype(ml_dtypes.bfloat16)


def order_table(size, parts, per_dev):
    width = size // parts
    out = np.zeros((per_dev, size, parts, per_dev, width), np.float32)
    for p in range(per_dev):
        for y in range(size):
            out[p, y, y % parts, p, y // parts] = 1.0
    return out.reshape(per_dev * size, parts * per_dev * width).astype(ml_dtypes.bfloat16)


def dot(a, b):
    return jnp.dot(a, b, preferred_element_type=F32)


def dot_nt(a, b):
    return lax.dot_general(a, b, (((1,), (1,)), ((), ())), preferred_element_type=F32)


def to_planes_kernel(c_ref, t_ref, o_hbm, out, first, second, sems):
    side = t_ref.shape[1] // 2
    devices = side // 4
    rows = first.shape[0] // devices
    blocks = rows // 2
    copies = []
    for n, scr in enumerate((first, second)):
        for g in range(blocks // 4):
            r = dot(c_ref[g * 256 : (g + 1) * 256, :], t_ref[:, n * side : (n + 1) * side])
            for i in range(4):
                part = r[i * 64 : (i + 1) * 64]
                part = jnp.concatenate([part[:, : side // 2], part[:, side // 2 :]], axis=0)
                part = jnp.transpose(part)
                for d in range(2):
                    at = pl.ds(d * blocks + g * 4 + i, devices, stride=rows)
                    scr[at, :] = part[d * devices : (d + 1) * devices]
        half = pl.ds(n * devices * rows, devices * rows)
        out[half, :] = scr[...].astype(BF16)
        copies.append(pltpu.make_async_copy(out.at[half], o_hbm.at[half], sems.at[n]))
        copies[-1].start()
    for copy in copies:
        copy.wait()


def from_planes_kernel(count, x_ref, t_ref, o_hbm, m_ref, scr, out, pairs0, pairs1, sems):
    devices = t_ref.shape[0] // 4
    rows = scr.shape[0] // devices
    blocks = rows // 2 - 1
    bands = m_ref.shape[2]
    scr[...] = x_ref[...].astype(F32)
    total = sum(scr[pl.ds(2 * blocks + i, devices, stride=rows), :] for i in range(2))
    total = jnp.sum(total, axis=0, keepdims=True) / count
    m_ref[0] = total[:, :bands]
    m_ref[1] = total[:, bands : 2 * bands]
    copies = []
    for g in range(blocks // 4):
        parts = []
        for m in range(g * 4, g * 4 + 4):
            y = jnp.concatenate(
                [scr[pl.ds(d * blocks + m, devices, stride=rows), :] for d in range(2)], axis=0
            )
            y = jnp.transpose(y).astype(BF16)
            parts.append(jnp.concatenate([y[:64], y[64:]], axis=1))
        value = dot(jnp.concatenate(parts, axis=0), t_ref[...])
        pairs = (pairs0, pairs1)[g % 2]
        for d in range(2):
            for k in range(2):
                at = d * 256 + k * 128
                pairs[pl.ds(2 * k + d, 256, stride=4), :] = value[:, at : at + 128]
        part = pl.ds(g * 1024, 1024)
        out[part, :] = pairs[...].astype(BF16)
        copies.append(pltpu.make_async_copy(out.at[part], o_hbm.at[part], sems.at[g]))
        copies[-1].start()
    for copy in copies:
        copy.wait()


def prepare_kernel(
    row_ref, col_ref, v_ref, f_ref, b_ref, ord_ref, tx_hbm, xt_hbm, v4_hbm, tx, xt, v4, sems
):
    size = f_ref.shape[0] // 2
    count = row_ref.shape[1]

    def hot(code, iota, s, axis):
        turn = (s * ((code >> 1) & 3) + (code & 1)) & 3
        hit = iota == (code >> 3)
        real = jnp.where(turn == 0, 1.0, jnp.where(turn == 2, -1.0, 0.0))
        imag = jnp.where(turn == 1, 1.0, jnp.where(turn == 3, -1.0, 0.0))
        return jnp.concatenate(
            [jnp.where(hit, real, 0.0), jnp.where(hit, imag, 0.0)], axis=axis
        ).astype(BF16)

    copies = []
    rows = lax.broadcasted_iota(jnp.int32, (size, count), 0)
    cols = lax.broadcasted_iota(jnp.int32, (count, size), 1)
    for s in range(4):
        part = slice(s * 2 * size, (s + 1) * 2 * size)
        tx[part, :] = dot(b_ref[...], hot(row_ref[...], rows, s, 0)).astype(BF16)
        copies.append(pltpu.make_async_copy(tx.at[part], tx_hbm.at[part], sems.at[s]))
        copies[-1].start()
        xt[:, part] = dot(hot(col_ref[...], cols, s, 1), f_ref[...]).astype(BF16)
    copies.append(pltpu.make_async_copy(xt, xt_hbm, sems.at[4]))
    copies[-1].start()
    v = jnp.concatenate([v_ref[0], v_ref[1]], axis=1)
    high = v.astype(BF16)
    rest = (v - high.astype(F32)).astype(BF16)
    both = dot(high, ord_ref[...]) + dot(rest, ord_ref[...])
    for s in range(4):
        v4[s] = both[:, s * 128 : (s + 1) * 128]
    copies.append(pltpu.make_async_copy(v4, v4_hbm, sems.at[5]))
    copies[-1].start()
    for copy in copies:
        copy.wait()


def planes_kernel(
    groups, r_ref, tx_hbm, xt_hbm, v4_hbm, yf_hbm, yb_hbm, o_ref,
    tx, xt, v4, yf, yb, h, r_scr, p_scr, stack, sems,
):
    size = v4.shape[1]
    bands, count = r_ref.shape[0], r_ref.shape[1]
    ffts = sum(groups)
    rows, blocks = count // ffts, count // ffts // 2
    message = o_ref.shape[0] // (bands * ffts)
    load_v = pltpu.make_async_copy(v4_hbm, v4, sems.at[5])
    load_f = pltpu.make_async_copy(yf_hbm, yf, sems.at[6])
    load_b = pltpu.make_async_copy(yb_hbm, yb, sems.at[7])
    loads = []
    quarters = []
    for i in range(4):
        part = slice(i * size // 2, (i + 1) * size // 2)
        quarters.append(pltpu.make_async_copy(tx_hbm.at[part], tx.at[part], sems.at[8 + i]))
    for s in range(1, 4):
        part = slice(s * 2 * size, (s + 1) * 2 * size)
        loads.append(pltpu.make_async_copy(tx_hbm.at[part], tx.at[part], sems.at[s]))
    load_xt = pltpu.make_async_copy(xt_hbm, xt, sems.at[4])
    for copy in quarters:
        copy.start()
    load_f.start()
    load_v.start()
    load_b.start()
    for copy in loads:
        copy.start()
    load_xt.start()
    for b in range(bands):
        r_scr[b * count : (b + 1) * count, :] = r_ref[b].astype(F32)

    for s in range(4):
        for copy in (quarters, [], loads[1:], [])[s]:
            copy.wait()
        w = jnp.concatenate([r_ref[b] for b in range(bands)], axis=1)
        g = dot(tx[s * 2 * size : (s + 1) * 2 * size, :], w).astype(BF16)
        left = jnp.concatenate(
            [
                jnp.concatenate(
                    [g[:size, b * 128 : (b + 1) * 128], g[size:, b * 128 : (b + 1) * 128]], axis=1
                )
                for b in range(bands)
            ],
            axis=0,
        )
        if s == 0:
            load_f.wait()
            load_v.wait()
            load_b.wait()
            loads[0].wait()
        v = jnp.concatenate([v4[s], v4[s]], axis=1)
        field = (dot(left, yf[s]) * jnp.concatenate([v] * bands, axis=0)).astype(BF16)
        back = dot(field, yb[s]).astype(BF16)
        row = s * 2 * size
        for b in range(bands):
            part = back[b * size : (b + 1) * size]
            h[row : row + size, b * 128 : (b + 1) * 128] = part[:, :128]
            h[row + size : row + 2 * size, b * 128 : (b + 1) * 128] = part[:, 128:]

    load_xt.wait()
    sums = {}

    def add(key, value):
        value = value[:8] + value[8:16] + value[16:24]
        sums[key] = sums[key] + value if key in sums else value

    first = 0
    for group in groups:
        for n in reversed(range(bands // 2)):
            out = dot(xt[first * rows : (first + group) * rows, :], h[:, n * 256 : (n + 1) * 256])
            for f in range(group):
                block = out[f * rows : (f + 1) * rows]
                for j in range(2):
                    at = ((2 * n + j) * ffts + first + f) * message
                    p_scr[at : at + rows, :] = block[:, j * 128 : (j + 1) * 128]
                for i in range(2 * n + 2):
                    at = i * count + (first + f) * rows
                    real, imag = r_scr[at : at + blocks, :], r_scr[at + blocks : at + rows, :]
                    for j in range(max(i, 2 * n), 2 * n + 2):
                        part = block[:, (j - 2 * n) * 128 : (j - 2 * n + 1) * 128]
                        add((i, j, 0), real * part[:blocks] + imag * part[blocks:])
                        add((i, j, 1), real * part[blocks:] - imag * part[:blocks])
            if first + group == ffts:
                for i, j, c in [key for key in sums if key[1] >= 2 * n]:
                    line = jnp.sum(sums.pop((i, j, c)), axis=0, keepdims=True)
                    at = (2 * i + c) * bands + j
                    stack[at : at + 1, :] = line
                    if i < j:
                        at = (2 * j + c) * bands + i
                        stack[at : at + 1, :] = -line if c else line
                done = slice(2 * n * ffts * message, (2 * n + 2) * ffts * message)
                o_ref[done, :] = p_scr[done, :].astype(BF16)
        first += group

    total = jnp.sum(jnp.transpose(stack[...]), axis=0, keepdims=True)
    high = total.astype(BF16).astype(F32)
    pair = jnp.concatenate([high, total - high], axis=0)
    for b in range(bands):
        part = pair if b == 0 else pltpu.roll(pair, 128 - b * 2 * bands, 1)
        part = part.astype(BF16)
        for f in range(ffts):
            at = (b * ffts + f) * message + rows
            o_ref[at : at + message - rows, :] = part


def call(kernel, out_shape, scratch, flops, args, in_hbm=(), out_hbm=(), limit=40):
    read = sum(a.size * a.dtype.itemsize for a in args)
    outs = out_shape if isinstance(out_shape, tuple) else (out_shape,)
    written = sum(math.prod(s.shape) * jnp.dtype(s.dtype).itemsize for s in outs)
    args = [
        pltpu.with_memory_space_constraint(a, pltpu.HBM) if i in in_hbm else a
        for i, a in enumerate(args)
    ]
    results = pl.pallas_call(
        kernel,
        out_shape=outs,
        in_specs=[HBM if i in in_hbm else VMEM for i in range(len(args))],
        out_specs=[HBM if i in out_hbm else VMEM for i in range(len(outs))],
        scratch_shapes=scratch,
        compiler_params=pltpu.CompilerParams(vmem_limit_bytes=limit * 2**20),
        cost_estimate=pl.CostEstimate(flops=flops, bytes_accessed=read + written, transcendentals=0),
    )(*args)
    return results if isinstance(out_shape, tuple) else results[0]


def body(coeffs, potential, pattern):
    block_count, block_width = coeffs.shape[1], coeffs.shape[2]
    size = coeffs.shape[-1]
    bands, ffts = lax.axis_size("band"), lax.axis_size("fft")
    devices = bands * ffts
    per_dev = size // devices
    sticks = block_count * block_width
    rows = 2 * block_count
    shape = jax.ShapeDtypeStruct

    table = plane_table(size, bands, ffts)
    halves = table.reshape(2 * per_dev, 2, devices // 2, 2 * size)
    halves = halves.transpose(1, 0, 2, 3).reshape(2 * size, 2 * size)
    forward = dft_table(size, 1.0).reshape(2 * size, 2 * size)
    y_forward = split_table(size, 4, per_dev)
    y_backward = np.ascontiguousarray(y_forward.transpose(0, 2, 1))

    sent = call(
        to_planes_kernel,
        pltpu.HBM((devices * rows, 128), BF16),
        [
            pltpu.VMEM((devices * rows, 128), BF16),
            pltpu.VMEM((devices * rows // 2, 128), F32),
            pltpu.VMEM((devices * rows // 2, 128), F32),
            pltpu.SemaphoreType.DMA((2,)),
        ],
        2 * sticks * (2 * size) ** 2,
        (coeffs.reshape(sticks, 2 * size), jnp.asarray(np.ascontiguousarray(halves.T))),
        out_hbm=(0,),
    )
    got = lax.all_to_all(
        sent.reshape(devices, rows, 128), AXES, split_axis=0, concat_axis=0, tiled=True
    )
    got = got.reshape(bands, ffts * rows, 128)

    order = pattern.reshape(ffts, 1, block_count) * 2 + jnp.arange(2, dtype=jnp.int32)[None, :, None]
    planes = lax.dynamic_slice_in_dim(potential, lax.axis_index("band") * per_dev, per_dev, 0)
    count = ffts * rows
    tables = (
        pltpu.HBM((8 * size, count), BF16),
        pltpu.HBM((count, 8 * size), BF16),
        pltpu.HBM((4, size, per_dev * size // 4), F32),
    )
    held = [pltpu.VMEM(t.shape, t.dtype) for t in tables]
    x_table, x_back, v4 = call(
        prepare_kernel,
        tables,
        held + [pltpu.SemaphoreType.DMA((6,))],
        2 * 2 * 4 * count * (2 * size) ** 2,
        (
            order.reshape(1, count),
            order.reshape(count, 1),
            planes,
            jnp.asarray(forward),
            jnp.asarray(np.ascontiguousarray(forward.T)),
            jnp.asarray(order_table(size, 4, per_dev)),
        ),
        out_hbm=(0, 1, 2),
    )

    message = rows + 2
    picked = call(
        functools.partial(planes_kernel, (16,)),
        shape((devices * message, 128), BF16),
        held
        + [
            pltpu.VMEM(y_forward.shape, BF16),
            pltpu.VMEM(y_forward.shape, BF16),
            pltpu.VMEM((8 * size, bands * 128), BF16),
            pltpu.VMEM((bands * count, 128), F32),
            pltpu.VMEM((devices * message, 128), F32),
            pltpu.VMEM((2 * bands * bands, 128), F32),
            pltpu.SemaphoreType.DMA((12,)),
        ],
        2 * bands * 128 * 2 * 8 * size * count,
        (got, x_table, x_back, v4, jnp.asarray(y_forward), jnp.asarray(y_backward)),
        in_hbm=(1, 2, 3, 4, 5),
    )
    returned = lax.all_to_all(
        picked.reshape(devices, message // 2, 2, 128), AXES, split_axis=0, concat_axis=0, tiled=True
    )

    total_count = block_count * ffts * block_width * size
    images, matrix_rows = call(
        functools.partial(from_planes_kernel, total_count),
        (pltpu.HBM((4 * sticks, 128), BF16), shape((2, 1, bands), F32)),
        [
            pltpu.VMEM((devices * message, 128), F32),
            pltpu.VMEM((4 * sticks, 128), BF16),
        ]
        + [pltpu.VMEM((1024, 128), F32)] * 2
        + [pltpu.SemaphoreType.DMA((block_count // 4,))],
        2 * sticks * (2 * size) ** 2,
        (returned.reshape(devices * message, 128), jnp.asarray(table)),
        out_hbm=(0,),
    )
    images = images.reshape(sticks, 2, 2, 128).transpose(0, 2, 1, 3)
    return (images.reshape(coeffs.shape), matrix_rows)


def solution(mesh):
    placed = (P("band", "fft", None, None, None), P("fft", None, None), P())
    return jax.shard_map(
        body,
        mesh=mesh,
        in_specs=placed,
        out_specs=(P("band", "fft", None, None, None), P(None, "band", None)),
        check_vma=False,
    )
```
